256 devices in a mesh: dp: 8 (over z_hi, core), ctx: 32 (over x, z_lo, y).
Axes of the slice: x: 4, y: 4, z: 8 (z_hi: 4, z_lo: 2; z = z_hi * 2 + z_lo), core: 2. Of those that a mesh axis runs over, the one named last changes fastest.
Arguments:
- query_proj: bfloat16 [8, 4096, 1024], P('dp', 'ctx'), may hold values from -6 to 6
- key_proj: bfloat16 [8, 4096, 1024], P('dp', 'ctx'), may hold values from -6 to 6
- value_proj: bfloat16 [8, 4096, 1024], P('dp', 'ctx'), may hold values from -6 to 6
- out_grad: bfloat16 [8, 4096, 1024], P('dp', 'ctx'), may hold values from -6 to 6
- filter_taps: float32 [4096, 1024], P(None, 'ctx'), may hold values from -0.09375 to 0.09375
Outputs:
- query_grad: bfloat16 [8, 4096, 1024], P('dp', 'ctx')
- key_grad: bfloat16 [8, 4096, 1024], P('dp', 'ctx')
- value_grad: bfloat16 [8, 4096, 1024], P('dp', 'ctx')
- taps_grad: float32 [4096, 1024], P('dp', 'ctx')
The draws below stay inside these ranges and needn't reach their ends.
All inputs are finite; a program needn't handle non-finite values.
Results may differ from the reference program's by a relative error of at most 0.0058.
Values may be sent and summed in bfloat16 or wider, within the bound.
A program may use at most 64 MiB of HBM per device.

```python
import math
import jax
import jax.numpy as jnp
from jax import lax

C = 1024
L = 4096
B = 8


def block_levels(rng, extent, shards, least, top_value):
    factor_of = 1.0
    for position, blocks in shards:
        heights = jax.random.uniform(jax.random.fold_in(jax.random.fold_in(rng, 6), position), (blocks,), jnp.float32, least / len(shards), top_value / len(shards))
        factor_of = factor_of * jnp.repeat(jnp.exp(heights), extent[position] // blocks).reshape((-1,) + (1,) * (len(extent) - 1 - position))
    return factor_of


def scatter_about(stream_key, dims, spread, most, split=(), kind=jnp.bfloat16):
    entries = spread * jax.random.normal(stream_key, dims, jnp.float32)
    if split:
        entries = entries * block_levels(stream_key, dims, split, -0.22, 0.18)
    return jnp.clip(entries, -most, most).astype(kind)


def setup_inputs(seed: int = 0) -> dict:
    splits = jax.random.split(jax.random.key(seed), 6)
    return {
        "query_proj": scatter_about(splits[0], (B, L, C), 1.0, 6.0, ((0, 8), (1, 32))),
        "key_proj": scatter_about(splits[1], (B, L, C), 1.0, 6.0, ((0, 8), (1, 32))),
        "value_proj": scatter_about(splits[2], (B, L, C), 1.0, 6.0, ((0, 8), (1, 32))),
        "out_grad": scatter_about(splits[3], (B, L, C), 1.0, 6.0, ((0, 8), (1, 32))),
        "filter_taps": scatter_about(splits[4], (L, C), (1.5 / L ** 0.5), 0.09375, ((1, 32),), jnp.float32),
    }


def reference(query_proj, key_proj, value_proj, out_grad, filter_taps):
    length = L
    padded_len = 2 * length
    kernel_spec = jnp.fft.fft(filter_taps, n=padded_len, axis=0)

    def one_sequence(running, items):
        query_row, key_row, value_row, grad_row = items
        product = (key_row.astype(jnp.float32) * value_row.astype(jnp.float32)).astype(jnp.bfloat16)
        mixed = (grad_row.astype(jnp.float32) * query_row.astype(jnp.float32)).astype(jnp.bfloat16)
        product_spec = jnp.fft.fft(product.astype(jnp.float32), n=padded_len, axis=0)
        mixed_spec = jnp.fft.fft(mixed.astype(jnp.float32), n=padded_len, axis=0)
        convolved = jnp.real(jnp.fft.ifft(kernel_spec * product_spec, axis=0))[:length].astype(jnp.bfloat16)
        query_grad = (grad_row.astype(jnp.float32) * convolved.astype(jnp.float32)).astype(jnp.bfloat16)
        inner_grad = jnp.real(jnp.fft.ifft(mixed_spec * jnp.conj(kernel_spec), axis=0))[:length]
        inner_grad = inner_grad.astype(jnp.bfloat16)
        key_grad = (inner_grad.astype(jnp.float32) * value_row.astype(jnp.float32)).astype(jnp.bfloat16)
        value_grad = (inner_grad.astype(jnp.float32) * key_row.astype(jnp.float32)).astype(jnp.bfloat16)
        kernel_term = jnp.real(jnp.fft.ifft(mixed_spec * jnp.conj(product_spec), axis=0))[:length]
        return (running + kernel_term, (query_grad, key_grad, value_grad))
    start = jnp.zeros((length, filter_taps.shape[1]), jnp.float32)
    kernel_grad, grads = lax.scan(one_sequence, start, (query_proj, key_proj, value_proj, out_grad))
    taps_grad = kernel_grad * (1.0 / math.sqrt(B * length))
    return (grads[0], grads[1], grads[2], taps_grad)
```

```python
import functools
import math

import jax
import jax.numpy as jnp
import ml_dtypes
import numpy as np
from jax import lax
from jax.experimental import pallas as pl
from jax.experimental.pallas import tpu as pltpu
from jax.sharding import PartitionSpec as P

MESH = pl.DeviceIdType.MESH
F32 = jnp.float32
BF16 = jnp.bfloat16

N1 = 32
N2 = 128
LENGTH = N1 * N2
GROUP = 4


def high_low(table):
    high = table.astype(ml_dtypes.bfloat16)
    low = (table - high.astype(np.float64)).astype(ml_dtypes.bfloat16)
    return high, low


@functools.lru_cache(maxsize=None)
def tables():
    row = np.arange(N1)
    col = np.arange(N2)
    outer = 2 * np.pi * np.outer(row + 0.25, row) / N1
    first = np.concatenate([np.cos(outer), -np.sin(outer)], axis=0)
    first_high, first_low = high_low(first)
    first_both = np.concatenate([first_high, first_low], axis=1)
    last = np.concatenate([np.cos(outer.T), -np.sin(outer.T)], axis=1) / LENGTH
    last_high, last_low = high_low(last)
    last_all = np.concatenate([last_high, last_high, last_low], axis=1)
    turn = 2 * np.pi * np.outer(row + 0.25, col) / LENGTH
    twist = np.stack([np.cos(turn), -np.sin(turn)]).astype(np.float32)
    inner = 2 * np.pi * (np.outer(col, col) % N2) / N2
    cos, sin = np.cos(inner), np.sin(inner)
    forward = np.block([[cos, -sin], [sin, cos]])
    inverse = np.block([[cos, sin], [-sin, cos]])
    stacked = np.stack(high_low(forward) + high_low(inverse))
    return first_both, last_all, twist, stacked


def place():
    dp = lax.axis_index("dp")
    ctx = lax.axis_index("ctx")
    return dp // 2, dp % 2, ctx


def peer_of(step, core, ctx):
    off = step // 2
    x, z, y = ctx // 8, (ctx // 4) % 2, ctx % 4
    there = ((x + off // 8) % 4) * 8 + ((z + (off // 4) % 2) % 2) * 4 + (y + off % 4) % 4
    return (core + step % 2) % 2, there


def send_kernel(query, key, value, grad, landed, packed, local_sem, send_sem, recv_sem):
    z_hi, core, ctx = place()
    barrier = pltpu.get_barrier_semaphore()

    def greet(step, carry):
        core_to, ctx_to = peer_of(step, core, ctx)
        pl.semaphore_signal(barrier, inc=1, device_id=(z_hi * 2 + core_to, ctx_to), device_id_type=MESH)
        return carry

    lax.fori_loop(1, 64, greet, 0)

    for block in range(8):
        lanes = slice(128 * block, 128 * block + 128)
        for array, (first, second) in enumerate(((key, value), (grad, query))):
            gated = first[:, lanes].astype(F32) * second[:, lanes].astype(F32)
            turned = gated.T.astype(BF16)
            for part in range(8):
                packed[4 * block + part // 2, part % 2, array] = turned[16 * part : 16 * part + 16]

    pl.semaphore_wait(barrier, 63)
    own = pltpu.make_async_copy(packed.at[ctx, core], landed.at[ctx, core], local_sem)
    own.start()

    def copy_to(step):
        core_to, ctx_to = peer_of(step, core, ctx)
        return pltpu.make_async_remote_copy(
            src_ref=packed.at[ctx_to, core_to],
            dst_ref=landed.at[ctx, core],
            send_sem=send_sem.at[step],
            recv_sem=recv_sem.at[ctx * 2 + core],
            device_id=(z_hi * 2 + core_to, ctx_to),
            device_id_type=MESH,
        )

    def send(step, carry):
        copy_to(step).start()
        return carry

    lax.fori_loop(1, 64, send, 0)

    def receive(step, carry):
        core_to, ctx_to = peer_of(step, core, ctx)
        pltpu.make_async_remote_copy(
            src_ref=packed.at[ctx_to, core_to],
            dst_ref=landed.at[ctx_to, core_to],
            send_sem=send_sem.at[step],
            recv_sem=recv_sem.at[ctx_to * 2 + core_to],
            device_id=(z_hi * 2 + core_to, ctx_to),
            device_id_type=MESH,
        ).wait()
        return carry

    lax.fori_loop(1, 64, receive, 0)
    own.wait()


def split(value):
    high = value.astype(BF16)
    return high, (value - high.astype(F32)).astype(BF16)


def dot(left, right):
    return lax.dot_general(left, right, (((1,), (0,)), ((), ())), preferred_element_type=F32)


def middle(value, high, low):
    value_high, value_low = split(value)
    return dot(value_high, high) + dot(value_low, high) + dot(value_high, low)


def twisted(value, twist):
    re, im = value[:N1], value[N1:]
    return jnp.concatenate([re * twist[0] - im * twist[1], re * twist[1] + im * twist[0]], axis=1)


def untwisted(value, twist):
    re, im = value[:, :N2], value[:, N2:]
    return jnp.concatenate([re * twist[0] + im * twist[1], im * twist[0] - re * twist[1]], axis=0)


def convolve_kernel(
    scale, landed, taps, first_both, last_all, twist_ref, mats, back, kernel_part, signals, filters, spectra, results, sums
):
    core = lax.axis_index("dp") % 2
    twist = (twist_ref[0], twist_ref[1])

    def unpack(n1, carry):
        signals[pl.ds(pl.multiple_of(n1 * 64, 64), 64)] = landed[n1].reshape(64, N2).astype(F32)
        rows = taps[pl.ds(pl.multiple_of(n1 * N2, N2), N2)].T
        filters[pl.ds(pl.multiple_of(n1 * 16, 16), 16)] = jnp.where(core == 0, rows[:16], rows[16:])
        return carry

    lax.fori_loop(0, N1, unpack, 0)

    def work(group, carry):
        forward = []
        for pair in range(GROUP // 2):
            channels = [group * GROUP + 2 * pair, group * GROUP + 2 * pair + 1]
            rows = [filters[pl.ds(c, N1, stride=16)] for c in channels]
            high, low = split(jnp.concatenate(rows, axis=1))
            left = first_both[...]
            out = dot(left, jnp.concatenate([high, high], axis=0)) + dot(left[:, :N1], low)
            forward += [twisted(out[:, :N2], twist), twisted(out[:, N2:], twist)]
        for item in range(GROUP):
            c = group * GROUP + item
            for pair in range(2):
                rows = [signals[pl.ds(c + 16 * (2 * s + pair), N1, stride=64)] for s in range(2)]
                data = jnp.concatenate(rows, axis=1).astype(BF16)
                out = dot(first_both[...], jnp.concatenate([data, data], axis=0))
                forward += [twisted(out[:, :N2], twist), twisted(out[:, N2:], twist)]
        spectra[...] = middle(jnp.concatenate(forward, axis=0), mats[0], mats[1])

        def spectrum(index):
            block = spectra[N1 * index : N1 * index + N1]
            return block[:, :N2], block[:, N2:]

        inverse = []
        for item in range(GROUP):
            h_re, h_im = spectrum(item)
            w_re, w_im = 0.0, 0.0
            for s in range(2):
                u_re, u_im = spectrum(GROUP + 4 * item + s)
                m_re, m_im = spectrum(GROUP + 4 * item + 2 + s)
                inverse.append(jnp.concatenate([h_re * u_re - h_im * u_im, h_re * u_im + h_im * u_re], axis=1))
                inverse.append(jnp.concatenate([m_re * h_re + m_im * h_im, m_im * h_re - m_re * h_im], axis=1))
                w_re = w_re + m_re * u_re + m_im * u_im
                w_im = w_im + m_im * u_re - m_re * u_im
            inverse.append(jnp.concatenate([w_re, w_im], axis=1))
        results[...] = middle(jnp.concatenate(inverse, axis=0), mats[2], mats[3])

        def finish(indices):
            turned = [untwisted(results[N1 * i : N1 * i + N1], twist) for i in indices]
            high, low = split(jnp.concatenate(turned, axis=1))
            out = dot(last_all[...], jnp.concatenate([high, low, high], axis=0))
            return out[:, :N2], out[:, N2:]

        for item in range(GROUP):
            c = group * GROUP + item
            for s in range(2):
                conv, inner = finish((5 * item + 2 * s, 5 * item + 2 * s + 1))
                signals[pl.ds(c + 32 * s, N1, stride=64)] = conv
                signals[pl.ds(c + 32 * s + 16, N1, stride=64)] = inner
        for pair in range(GROUP // 2):
            c = group * GROUP + 2 * pair
            parts = finish((10 * pair + 4, 10 * pair + 9))
            sums[pl.ds(c, N1, stride=16)] = parts[0] * scale
            sums[pl.ds(c + 1, N1, stride=16)] = parts[1] * scale
        return carry

    lax.fori_loop(0, 16 // GROUP, work, 0)

    def pack(n1, carry):
        rows = signals[pl.ds(pl.multiple_of(n1 * 64, 64), 64)].astype(BF16)
        back[n1] = rows.reshape(2, 2, 16, N2)
        kernel_part[n1] = sums[pl.ds(pl.multiple_of(n1 * 16, 16), 16)].astype(BF16)
        return carry

    lax.fori_loop(0, N1, pack, 0)


def return_kernel(back, kernel_part, landed, gathered, local_sem, send_sem, recv_sem, part_send, part_recv):
    z_hi, core, ctx = place()
    barrier = pltpu.get_barrier_semaphore()

    def greet(step, carry):
        core_to, ctx_to = peer_of(step, core, ctx)
        pl.semaphore_signal(barrier, inc=1, device_id=(z_hi * 2 + core_to, ctx_to), device_id_type=MESH)
        return carry

    lax.fori_loop(1, 64, greet, 0)

    def greet_far(step, carry):
        z_to, core_to = (z_hi + step // 2) % 4, (core + step % 2) % 2
        pl.semaphore_signal(barrier, inc=1, device_id=(z_to * 2 + core_to, ctx), device_id_type=MESH)
        return carry

    lax.fori_loop(2, 8, greet_far, 0)
    pl.semaphore_wait(barrier, 69)

    def part_copy(step, here):
        z_to, core_to = (z_hi + step // 2) % 4, (core + step % 2) % 2
        to = z_to * 2 + core_to
        slot_z, slot_core = (z_hi, core) if here else (z_to, core_to)
        return pltpu.make_async_remote_copy(
            src_ref=kernel_part.at[pl.ds(to * 4, 4)],
            dst_ref=gathered.at[slot_core, slot_z],
            send_sem=part_send.at[step],
            recv_sem=part_recv.at[slot_z * 2 + slot_core],
            device_id=(to, ctx),
            device_id_type=MESH,
        )

    def copy(step, here):
        core_to, ctx_to = peer_of(step, core, ctx)
        slot_core, slot_ctx = (core, ctx) if here else (core_to, ctx_to)
        return pltpu.make_async_remote_copy(
            src_ref=back.at[ctx_to, core_to],
            dst_ref=landed.at[:, slot_ctx, slot_core],
            send_sem=send_sem.at[step],
            recv_sem=recv_sem.at[slot_ctx * 2 + slot_core],
            device_id=(z_hi * 2 + core_to, ctx_to),
            device_id_type=MESH,
        )

    def start_part(step, carry):
        part_copy(step, True).start()
        return carry

    def start(step, carry):
        copy(step, True).start()
        return carry

    lax.fori_loop(1, 8, start_part, 0)
    lax.fori_loop(1, 64, start, 0)
    own = pltpu.make_async_copy(back.at[ctx, core], landed.at[:, ctx, core], local_sem.at[0])
    own_part = pltpu.make_async_copy(
        kernel_part.at[pl.ds((z_hi * 2 + core) * 4, 4)], gathered.at[core, z_hi], local_sem.at[1]
    )
    own.start()
    own_part.start()

    def finish(step, carry):
        copy(step, False).wait()
        return carry

    def finish_part(step, carry):
        part_copy(step, False).wait()
        return carry

    lax.fori_loop(1, 64, finish, 0)
    lax.fori_loop(1, 8, finish_part, 0)
    own.wait()
    own_part.wait()


def gate_kernel(landed, gathered, query, key, value, grad, query_grad, key_grad, value_grad, taps_grad):
    for block in range(8):
        lanes = slice(128 * block, 128 * block + 128)
        conv = landed[0, 4 * block : 4 * block + 4].reshape(128, N2).astype(F32).T
        inner = landed[1, 4 * block : 4 * block + 4].reshape(128, N2).astype(F32).T
        query_grad[:, lanes] = (conv * grad[:, lanes].astype(F32)).astype(BF16)
        key_grad[:, lanes] = (inner * value[:, lanes].astype(F32)).astype(BF16)
        value_grad[:, lanes] = (inner * key[:, lanes].astype(F32)).astype(BF16)
    for n1 in range(4):
        total = gathered[0, 0, n1].astype(F32), gathered[1, 0, n1].astype(F32)
        for z in range(1, 4):
            total = (total[0] + gathered[0, z, n1].astype(F32), total[1] + gathered[1, z, n1].astype(F32))
        taps_grad[128 * n1 : 128 * n1 + 128] = jnp.concatenate(total, axis=0).T


def on_device(query_proj, key_proj, value_proj, out_grad, filter_taps):
    rows = query_proj.shape[1]
    query, key, value, grad = (a.reshape(rows, -1) for a in (query_proj, key_proj, value_proj, out_grad))
    vmem = pl.BlockSpec(memory_space=pltpu.VMEM)
    limit = 48 * 1024 * 1024
    slabs = jax.ShapeDtypeStruct((N1, 2, 2, 16, N2), BF16)
    landed = pl.pallas_call(
        send_kernel,
        out_shape=slabs,
        in_specs=[vmem] * 4,
        out_specs=vmem,
        scratch_shapes=[
            pltpu.VMEM((N1, 2, 2, 16, N2), BF16),
            pltpu.SemaphoreType.DMA,
            pltpu.SemaphoreType.DMA((64,)),
            pltpu.SemaphoreType.DMA((64,)),
        ],
        compiler_params=pltpu.CompilerParams(collective_id=0, has_side_effects=True, vmem_limit_bytes=limit),
        name="send_gated",
    )(query, key, value, grad)
    scale = 1.0 / math.sqrt(lax.axis_size("dp") * LENGTH)
    back, kernel_part = pl.pallas_call(
        functools.partial(convolve_kernel, scale),
        out_shape=(slabs, jax.ShapeDtypeStruct((N1, 16, N2), BF16)),
        in_specs=[vmem] * 6,
        out_specs=(vmem, vmem),
        scratch_shapes=[
            pltpu.VMEM((N1 * 64, N2), F32),
            pltpu.VMEM((N1 * 16, N2), F32),
            pltpu.VMEM((5 * GROUP * N1, 2 * N2), F32),
            pltpu.VMEM((5 * GROUP * N1, 2 * N2), F32),
            pltpu.VMEM((N1 * 16, N2), F32),
        ],
        compiler_params=pltpu.CompilerParams(vmem_limit_bytes=limit),
        name="convolve",
    )(landed, filter_taps, *(jnp.asarray(t) for t in tables()))
    returned, gathered = pl.pallas_call(
        return_kernel,
        out_shape=(
            jax.ShapeDtypeStruct((2, N1, 2, 16, N2), BF16),
            jax.ShapeDtypeStruct((2, 4, 4, 16, N2), BF16),
        ),
        in_specs=[vmem] * 2,
        out_specs=(vmem, vmem),
        scratch_shapes=[
            pltpu.SemaphoreType.DMA((2,)),
            pltpu.SemaphoreType.DMA((64,)),
            pltpu.SemaphoreType.DMA((64,)),
            pltpu.SemaphoreType.DMA((8,)),
            pltpu.SemaphoreType.DMA((8,)),
        ],
        compiler_params=pltpu.CompilerParams(collective_id=1, has_side_effects=True, vmem_limit_bytes=limit),
        name="send_back",
    )(back, kernel_part)
    flat = jax.ShapeDtypeStruct(query.shape, BF16)
    outs = pl.pallas_call(
        gate_kernel,
        out_shape=(flat, flat, flat, jax.ShapeDtypeStruct((4 * N2, 32), F32)),
        in_specs=[vmem] * 6,
        out_specs=(vmem,) * 4,
        compiler_params=pltpu.CompilerParams(vmem_limit_bytes=limit),
        name="gate",
    )(returned, gathered, query, key, value, grad)
    return tuple(o.reshape(query_proj.shape) for o in outs[:3]) + (outs[3],)


def solution(mesh):
    placed = (P("dp", "ctx", None),) * 4 + (P(None, "ctx"),)
    return jax.shard_map(
        on_device,
        mesh=mesh,
        in_specs=placed,
        out_specs=(P("dp", "ctx", None),) * 3 + (P("dp", "ctx"),),
        check_vma=False,
    )
```

```python
import functools
import math

import jax
import jax.numpy as jnp
import ml_dtypes
import numpy as np
from jax import lax
from jax.experimental import pallas as pl
from jax.experimental.pallas import tpu as pltpu
from jax.sharding import PartitionSpec as P

MESH = pl.DeviceIdType.MESH
F32 = jnp.float32
BF16 = jnp.bfloat16

N1 = 32
N2 = 128
LENGTH = N1 * N2
GROUP = 8
HALF = 16


def high_low(table):
    high = table.astype(ml_dtypes.bfloat16)
    low = (table - high.astype(np.float64)).astype(ml_dtypes.bfloat16)
    return high, low


@functools.lru_cache(maxsize=None)
def tables():
    row = np.arange(N1)
    col = np.arange(N2)
    outer = 2 * np.pi * np.outer(row + 0.25, row) / N1
    first = np.concatenate([np.cos(outer), -np.sin(outer)], axis=0)
    first_high, first_low = high_low(first)
    first_both = np.concatenate([first_high, first_low], axis=1)
    last = np.concatenate([np.cos(outer.T), -np.sin(outer.T)], axis=1) / LENGTH
    last_high, last_low = high_low(last)
    last_all = np.concatenate([last_high, last_high, last_low], axis=1)
    turn = 2 * np.pi * np.outer(row + 0.25, col) / LENGTH
    twist = np.stack([np.cos(turn), -np.sin(turn)]).astype(np.float32)
    inner = 2 * np.pi * (np.outer(col, col) % N2) / N2
    cos, sin = np.cos(inner), np.sin(inner)
    forward = np.block([[cos, -sin], [sin, cos]])
    inverse = np.block([[cos, sin], [-sin, cos]])
    stacked = np.stack(high_low(forward) + high_low(inverse))
    return first_both, last_all, twist, stacked


def place():
    dp = lax.axis_index("dp")
    ctx = lax.axis_index("ctx")
    return dp // 2, dp % 2, ctx


def gray(j):
    return j + (j // 2) * (1 - 2 * (j % 2))


def peer_of(step, ctx):
    x, z, y = ctx // 8, (ctx // 4) % 2, ctx % 4
    return ((x + gray(step // 8)) % 4) * 8 + ((z + step % 2) % 2) * 4 + (y + gray((step // 2) % 4)) % 4


def split(value):
    high = value.astype(BF16)
    return high, (value - high.astype(F32)).astype(BF16)


def dot(left, right):
    return lax.dot_general(left, right, (((1,), (0,)), ((), ())), preferred_element_type=F32)


def middle(value, high, low):
    value_high, value_low = split(value)
    return dot(value_high, high) + dot(value_low, high) + dot(value_high, low)


def twisted(value, twist):
    re, im = value[:N1], value[N1:]
    return jnp.concatenate([re * twist[0] - im * twist[1], re * twist[1] + im * twist[0]], axis=1)


def untwisted(value, twist):
    re, im = value[:, :N2], value[:, N2:]
    return jnp.concatenate([re * twist[0] + im * twist[1], im * twist[0] - re * twist[1]], axis=0)


def fused_kernel(
    scale, query_hbm, key_hbm, value_hbm, grad_hbm, taps, first_both, last_all, twist_ref, mats, landed, gathered,
    inputs, packed, arrived, back, signals, filters, filter_spectra, spectra, results, sums, pair_sums, parts,
    load_sem, out_send, out_recv, back_send, back_recv, own_sem, pair_send, pair_recv, part_send, part_recv,
):
    z_hi, core, ctx = place()
    dp = z_hi * 2 + core
    pair = (z_hi * 2 + (core + 1) % 2, ctx)
    loads = [
        pltpu.make_async_copy(ref, inputs.at[i], load_sem.at[i])
        for i, ref in enumerate((key_hbm, value_hbm, grad_hbm, query_hbm))
    ]
    for load in loads:
        load.start()

    barrier = pltpu.get_barrier_semaphore()

    def greet(step, carry):
        pl.semaphore_signal(barrier, inc=1, device_id=(dp, peer_of(step, ctx)), device_id_type=MESH)
        return carry

    lax.fori_loop(1, 32, greet, 0)
    pl.semaphore_signal(barrier, inc=1, device_id=pair, device_id_type=MESH)
    for away in range(1, 4):
        there = ((z_hi + away) % 4) * 2 + core
        pl.semaphore_signal(barrier, inc=1, device_id=(there, ctx), device_id_type=MESH)

    def out_copy(half, there, slot):
        return pltpu.make_async_remote_copy(
            src_ref=packed.at[there, half],
            dst_ref=arrived.at[slot, half],
            send_sem=out_send.at[half, there],
            recv_sem=out_recv.at[half, slot],
            device_id=(dp, there),
            device_id_type=MESH,
        )

    def back_copy(half, there, slot):
        return pltpu.make_async_remote_copy(
            src_ref=back.at[there, half],
            dst_ref=landed.at[slot, half],
            send_sem=back_send.at[half, there],
            recv_sem=back_recv.at[half, slot],
            device_id=(dp, there),
            device_id_type=MESH,
        )

    def pair_copy(half, z):
        return pltpu.make_async_remote_copy(
            src_ref=sums.at[half, pl.ds((z * 2 + (core + 1) % 2) * 64, 64)],
            dst_ref=pair_sums.at[half, z],
            send_sem=pair_send.at[half, z],
            recv_sem=pair_recv.at[half, z],
            device_id=pair,
            device_id_type=MESH,
        )

    def part_copy(half, there, slot):
        return pltpu.make_async_remote_copy(
            src_ref=parts.at[half, there],
            dst_ref=gathered.at[half, slot],
            send_sem=part_send.at[half, there],
            recv_sem=part_recv.at[half, slot],
            device_id=(there * 2 + core, ctx),
            device_id_type=MESH,
        )

    def steps(body):
        def run(step, carry):
            body(peer_of(31 - step, ctx))
            return carry

        lax.fori_loop(0, 31, run, 0)

    for load in loads:
        load.wait()
    x, z_lo = ctx // 8, (ctx // 4) % 2
    for order, (dx, dz) in enumerate(((2, 1), (2, 0), (1, 1), (3, 1), (1, 0), (3, 0), (0, 1), (0, 0))):
        block = ((x + dx) % 4) * 2 + (z_lo + dz) % 2
        lanes = pl.ds(pl.multiple_of(128 * block, 128), 128)
        for array in range(2):
            gated = inputs[2 * array, :, lanes].astype(F32) * inputs[2 * array + 1, :, lanes].astype(F32)
            turned = gated.T.astype(BF16)
            for part in range(8):
                packed[4 * block + part // 2, part % 2, array] = turned[16 * part : 16 * part + 16]
        if order == 0:
            pl.semaphore_wait(barrier, 35)
        for dy in (2, 1, 3, 0):
            if dx or dz or dy:
                there = 4 * block + (ctx + dy) % 4
                out_copy(0, there, ctx).start()
    own = [
        pltpu.make_async_copy(packed.at[ctx, half], arrived.at[ctx, half], own_sem.at[half]) for half in range(2)
    ]
    own[0].start()
    own[1].start()
    steps(lambda there: out_copy(1, there, ctx).start())

    twist = (twist_ref[0], twist_ref[1])
    for n1 in range(N1):
        filters[32 * n1 : 32 * n1 + 32] = taps[:, N2 * n1 : N2 * n1 + N2]

    def filter_work(group, carry):
        forward = []
        for item in range(0, GROUP, 2):
            rows = [filters[pl.ds(group * GROUP + item + i, N1, stride=32)] for i in range(2)]
            high, low = split(jnp.concatenate(rows, axis=1))
            left = first_both[...]
            out = dot(left, jnp.concatenate([high, high], axis=0)) + dot(left[:, :N1], low)
            forward += [twisted(out[:, :N2], twist), twisted(out[:, N2:], twist)]
        rows = pl.ds(pl.multiple_of(group * GROUP * N1, GROUP * N1), GROUP * N1)
        filter_spectra[rows] = middle(jnp.concatenate(forward, axis=0), mats[0], mats[1])
        return carry

    lax.fori_loop(0, 2 * HALF // GROUP, filter_work, 0)

    for half in range(2):
        steps(lambda there: out_copy(half, there, there).wait_recv())
        own[half].wait()

        def unpack(n1, carry):
            rows = arrived[n1, half].reshape(32, N2).astype(F32)
            signals[pl.ds(pl.multiple_of(n1 * 32, 32), 32)] = rows
            return carry

        lax.fori_loop(0, N1, unpack, 0)

        def work(group, carry):
            forward = []
            for item in range(GROUP):
                rows = [signals[pl.ds(group * GROUP + item + HALF * i, N1, stride=32)] for i in range(2)]
                data = jnp.concatenate(rows, axis=1).astype(BF16)
                out = dot(first_both[...], jnp.concatenate([data, data], axis=0))
                forward += [twisted(out[:, :N2], twist), twisted(out[:, N2:], twist)]
            spectra[...] = middle(jnp.concatenate(forward, axis=0), mats[0], mats[1])
            inverse = []
            for item in range(GROUP):
                start = (half * HALF + group * GROUP + item) * N1
                h = filter_spectra[pl.ds(pl.multiple_of(start, N1), N1)]
                h_re, h_im = h[:, :N2], h[:, N2:]
                u = spectra[2 * item * N1 : (2 * item + 1) * N1]
                u_re, u_im = u[:, :N2], u[:, N2:]
                m = spectra[(2 * item + 1) * N1 : (2 * item + 2) * N1]
                m_re, m_im = m[:, :N2], m[:, N2:]
                inverse.append(jnp.concatenate([h_re * u_re - h_im * u_im, h_re * u_im + h_im * u_re], axis=1))
                inverse.append(jnp.concatenate([m_re * h_re + m_im * h_im, m_im * h_re - m_re * h_im], axis=1))
                inverse.append(jnp.concatenate([m_re * u_re + m_im * u_im, m_im * u_re - m_re * u_im], axis=1))
            results[...] = middle(jnp.concatenate(inverse, axis=0), mats[2], mats[3])

            def finish(indices):
                turned = [untwisted(results[N1 * i : N1 * i + N1], twist) for i in indices]
                high, low = split(jnp.concatenate(turned, axis=1))
                out = dot(last_all[...], jnp.concatenate([high, low, high], axis=0))
                return out[:, :N2], out[:, N2:]

            for item in range(GROUP):
                c = group * GROUP + item
                conv, inner = finish((3 * item, 3 * item + 1))
                signals[pl.ds(c, N1, stride=32)] = conv
                signals[pl.ds(c + HALF, N1, stride=32)] = inner
            for item in range(0, GROUP, 2):
                c = group * GROUP + item
                first, second = finish((3 * item + 2, 3 * item + 5))
                sums[half, pl.ds(c, N1, stride=HALF)] = first * scale
                sums[half, pl.ds(c + 1, N1, stride=HALF)] = second * scale
            return carry

        lax.fori_loop(0, HALF // GROUP, work, 0)

        def pack(n1, carry):
            rows = signals[pl.ds(pl.multiple_of(n1 * 32, 32), 32)].astype(BF16)
            back[n1, half] = rows.reshape(2, 16, N2)
            return carry

        lax.fori_loop(0, N1, pack, 0)
        for z in range(4):
            pair_copy(half, z).start()
        steps(lambda there: back_copy(half, there, ctx).start())
        landed[ctx, half] = back[ctx, half]
        for z in range(4):
            pair_copy(half, z).wait()
            mine = sums[half, pl.ds(pl.multiple_of((z * 2 + core) * 64, 64), 64)]
            parts[half, z] = (mine + pair_sums[half, z]).astype(BF16)
        for away in (2, 1, 3):
            part_copy(half, (z_hi + away) % 4, z_hi).start()
        gathered[half, z_hi] = parts[half, z_hi]

    for half in range(2):
        steps(lambda there: out_copy(half, there, there).wait_send())
        steps(lambda there: back_copy(half, there, there).wait())
        for away in (2, 1, 3):
            there = (z_hi + away) % 4
            part_copy(half, there, there).wait()


def gate_kernel(landed, gathered, query, key, value, grad, query_grad, key_grad, value_grad, taps_grad):
    for block in range(8):
        lanes = slice(128 * block, 128 * block + 128)
        devices = slice(4 * block, 4 * block + 4)
        conv = landed[devices, :, 0].reshape(128, N2).astype(F32).T
        inner = landed[devices, :, 1].reshape(128, N2).astype(F32).T
        query_grad[:, lanes] = (conv * grad[:, lanes].astype(F32)).astype(BF16)
        key_grad[:, lanes] = (inner * value[:, lanes].astype(F32)).astype(BF16)
        value_grad[:, lanes] = (inner * key[:, lanes].astype(F32)).astype(BF16)
    for half in range(2):
        total = gathered[half, 0].astype(F32)
        for z in range(1, 4):
            total = total + gathered[half, z].astype(F32)
        for n1 in range(4):
            taps_grad[16 * half : 16 * half + 16, N2 * n1 : N2 * n1 + N2] = total[16 * n1 : 16 * n1 + 16]


def on_device(query_proj, key_proj, value_proj, out_grad, filter_taps):
    rows = query_proj.shape[1]
    query, key, value, grad = (a.reshape(rows, -1) for a in (query_proj, key_proj, value_proj, out_grad))
    vmem = pl.BlockSpec(memory_space=pltpu.VMEM)
    anywhere = pl.BlockSpec(memory_space=pl.ANY)
    limit = 40 * 1024 * 1024
    slabs = (N1, 2, 2, HALF, N2)
    scale = 1.0 / math.sqrt(lax.axis_size("dp") * LENGTH)
    dma = pltpu.SemaphoreType.DMA
    landed, gathered = pl.pallas_call(
        functools.partial(fused_kernel, scale),
        out_shape=(jax.ShapeDtypeStruct(slabs, BF16), jax.ShapeDtypeStruct((2, 4, 64, N2), BF16)),
        in_specs=[anywhere] * 4 + [vmem] * 5,
        out_specs=(vmem, vmem),
        scratch_shapes=[
            pltpu.VMEM((4, rows, query.shape[1]), BF16),
            pltpu.VMEM(slabs, BF16),
            pltpu.VMEM(slabs, BF16),
            pltpu.VMEM(slabs, BF16),
            pltpu.VMEM((N1 * 2 * HALF, N2), F32),
            pltpu.VMEM((N1 * 2 * HALF, N2), F32),
            pltpu.VMEM((2 * HALF * N1, 2 * N2), F32),
            pltpu.VMEM((2 * GROUP * N1, 2 * N2), F32),
            pltpu.VMEM((3 * GROUP * N1, 2 * N2), F32),
            pltpu.VMEM((2, N1 * HALF, N2), F32),
            pltpu.VMEM((2, 4, 64, N2), F32),
            pltpu.VMEM((2, 4, 64, N2), BF16),
            dma((4,)),
            dma((2, 32)),
            dma((2, 32)),
            dma((2, 32)),
            dma((2, 32)),
            dma((2,)),
            dma((2, 4)),
            dma((2, 4)),
            dma((2, 4)),
            dma((2, 4)),
        ],
        compiler_params=pltpu.CompilerParams(collective_id=0, has_side_effects=True, vmem_limit_bytes=limit),
        name="exchange_convolve",
    )(query, key, value, grad, filter_taps.T, *(jnp.asarray(t) for t in tables()))
    flat = jax.ShapeDtypeStruct(query.shape, BF16)
    outs = pl.pallas_call(
        gate_kernel,
        out_shape=(flat, flat, flat, jax.ShapeDtypeStruct((2 * HALF, 4 * N2), F32)),
        in_specs=[vmem] * 6,
        out_specs=(vmem,) * 4,
        compiler_params=pltpu.CompilerParams(vmem_limit_bytes=48 * 1024 * 1024),
        name="gate",
    )(landed, gathered, query, key, value, grad)
    return tuple(o.reshape(query_proj.shape) for o in outs[:3]) + (outs[3].T,)


def solution(mesh):
    placed = (P("dp", "ctx", None),) * 4 + (P(None, "ctx"),)
    return jax.shard_map(
        on_device,
        mesh=mesh,
        in_specs=placed,
        out_specs=(P("dp", "ctx", None),) * 3 + (P("dp", "ctx"),),
        check_vma=False,
    )
```

```python
import functools
import math

import jax
import jax.numpy as jnp
import ml_dtypes
import numpy as np
from jax import lax
from jax.experimental import pallas as pl
from jax.experimental.pallas import tpu as pltpu
from jax.sharding import PartitionSpec as P

MESH = pl.DeviceIdType.MESH
F32 = jnp.float32
BF16 = jnp.bfloat16

N1 = 32
N2 = 128
LENGTH = N1 * N2
GROUP = 8
HALF = 16


def high_low(table):
    high = table.astype(ml_dtypes.bfloat16)
    low = (table - high.astype(np.float64)).astype(ml_dtypes.bfloat16)
    return high, low


@functools.lru_cache(maxsize=None)
def tables():
    row = np.arange(N1)
    col = np.arange(N2)
    outer = 2 * np.pi * np.outer(row + 0.25, row) / N1
    first = np.concatenate([np.cos(outer), -np.sin(outer)], axis=0)
    first_high, first_low = high_low(first)
    first_both = np.concatenate([first_high, first_low], axis=1)
    last = np.concatenate([np.cos(outer.T), -np.sin(outer.T)], axis=1) / LENGTH
    last_high, last_low = high_low(last)
    last_all = np.concatenate([last_high, last_high, last_low], axis=1)
    turn = 2 * np.pi * np.outer(row + 0.25, col) / LENGTH
    twist = np.stack([np.cos(turn), -np.sin(turn)]).astype(np.float32)
    inner = 2 * np.pi * (np.outer(col, col) % N2) / N2
    cos, sin = np.cos(inner), np.sin(inner)
    forward = np.block([[cos, -sin], [sin, cos]])
    inverse = np.block([[cos, sin], [-sin, cos]])
    stacked = np.stack(high_low(forward) + high_low(inverse))
    return first_both, last_all, twist, stacked


def place():
    dp = lax.axis_index("dp")
    ctx = lax.axis_index("ctx")
    return dp // 2, dp % 2, ctx


def gray(j):
    return j + (j // 2) * (1 - 2 * (j % 2))


def peer_of(step, ctx):
    x, z, y = ctx // 8, (ctx // 4) % 2, ctx % 4
    return ((x + gray(step // 8)) % 4) * 8 + ((z + step % 2) % 2) * 4 + (y + gray((step // 2) % 4)) % 4


def split(value):
    high = value.astype(BF16)
    return high, (value - high.astype(F32)).astype(BF16)


def dot(left, right):
    return lax.dot_general(left, right, (((1,), (0,)), ((), ())), preferred_element_type=F32)


def middle(value, high, low):
    value_high, value_low = split(value)
    return dot(value_high, high) + dot(value_low, high) + dot(value_high, low)


def twisted(value, twist):
    re, im = value[:N1], value[N1:]
    return jnp.concatenate([re * twist[0] - im * twist[1], re * twist[1] + im * twist[0]], axis=1)


def untwisted(value, twist):
    re, im = value[:, :N2], value[:, N2:]
    return jnp.concatenate([re * twist[0] + im * twist[1], im * twist[0] - re * twist[1]], axis=0)


def fused_kernel(
    scale, query_hbm, key_hbm, value_hbm, grad_hbm, taps_hbm, first_hbm, last_hbm, twist_hbm, mats_hbm, landed,
    inputs, taps, first_both, last_all, twist_ref, mats, packed, arrived, back, signals, filters, filter_spectra, spectra, results, sums, pair_sums, parts,
    load_sem, out_send, out_recv, back_send, back_recv, own_sem, pair_send, pair_recv, part_send, part_recv,
):
    z_hi, core, ctx = place()
    dp = z_hi * 2 + core
    pair = (z_hi * 2 + (core + 1) % 2, ctx)
    loads = [
        pltpu.make_async_copy(ref, inputs.at[i], load_sem.at[i])
        for i, ref in enumerate((key_hbm, value_hbm, grad_hbm, query_hbm))
    ]
    later = ((taps_hbm, taps), (first_hbm, first_both), (last_hbm, last_all), (twist_hbm, twist_ref), (mats_hbm, mats))
    loads += [pltpu.make_async_copy(ref, held, load_sem.at[4 + i]) for i, (ref, held) in enumerate(later)]
    for load in loads:
        load.start()

    barrier = pltpu.get_barrier_semaphore()

    def greet(step, carry):
        pl.semaphore_signal(barrier, inc=1, device_id=(dp, peer_of(step, ctx)), device_id_type=MESH)
        return carry

    lax.fori_loop(1, 32, greet, 0)
    pl.semaphore_signal(barrier, inc=1, device_id=pair, device_id_type=MESH)
    for away in range(1, 4):
        there = ((z_hi + away) % 4) * 2 + core
        pl.semaphore_signal(barrier, inc=1, device_id=(there, ctx), device_id_type=MESH)

    def out_copy(half, there, slot):
        return pltpu.make_async_remote_copy(
            src_ref=packed.at[there, half],
            dst_ref=arrived.at[slot, half],
            send_sem=out_send.at[half, there],
            recv_sem=out_recv.at[half, slot],
            device_id=(dp, there),
            device_id_type=MESH,
        )

    def back_copy(half, there, slot):
        return pltpu.make_async_remote_copy(
            src_ref=back.at[there, half],
            dst_ref=landed.at[slot, half],
            send_sem=back_send.at[half, there],
            recv_sem=back_recv.at[half, slot],
            device_id=(dp, there),
            device_id_type=MESH,
        )

    def pair_copy(half, z):
        return pltpu.make_async_remote_copy(
            src_ref=sums.at[half, pl.ds((z * 2 + (core + 1) % 2) * 64, 64)],
            dst_ref=pair_sums.at[half, z],
            send_sem=pair_send.at[half, z],
            recv_sem=pair_recv.at[half, z],
            device_id=pair,
            device_id_type=MESH,
        )

    def part_copy(half, there, slot):
        return pltpu.make_async_remote_copy(
            src_ref=parts.at[half, there],
            dst_ref=landed.at[N1 + half * 4 + slot],
            send_sem=part_send.at[half, there],
            recv_sem=part_recv.at[half, slot],
            device_id=(there * 2 + core, ctx),
            device_id_type=MESH,
        )

    def steps(body):
        def run(step, carry):
            body(peer_of(31 - step, ctx))
            return carry

        lax.fori_loop(0, 31, run, 0)

    for load in loads[:4]:
        load.wait()
    x, z_lo = ctx // 8, (ctx // 4) % 2
    for order, (dx, dz) in enumerate(((2, 1), (2, 0), (1, 1), (3, 1), (1, 0), (3, 0), (0, 1), (0, 0))):
        block = ((x + dx) % 4) * 2 + (z_lo + dz) % 2
        lanes = pl.ds(pl.multiple_of(128 * block, 128), 128)
        for array in range(2):
            gated = inputs[2 * array, :, lanes].astype(F32) * inputs[2 * array + 1, :, lanes].astype(F32)
            turned = gated.T.astype(BF16)
            for part in range(8):
                packed[4 * block + part // 2, part % 2, array] = turned[16 * part : 16 * part + 16]
        if order == 0:
            pl.semaphore_wait(barrier, 35)
        for dy in (2, 1, 3, 0):
            if dx or dz or dy:
                there = 4 * block + (ctx + dy) % 4
                out_copy(0, there, ctx).start()
    own = [
        pltpu.make_async_copy(packed.at[ctx, half], arrived.at[ctx, half], own_sem.at[half]) for half in range(2)
    ]
    keep = [
        pltpu.make_async_copy(back.at[ctx, half], landed.at[ctx, half], own_sem.at[2 + half]) for half in range(2)
    ] + [
        pltpu.make_async_copy(parts.at[half, z_hi], landed.at[N1 + half * 4 + z_hi], own_sem.at[4 + half])
        for half in range(2)
    ]
    own[0].start()
    own[1].start()
    steps(lambda there: out_copy(1, there, ctx).start())

    for load in loads[4:]:
        load.wait()
    twist = (twist_ref[0], twist_ref[1])
    for n1 in range(N1):
        filters[32 * n1 : 32 * n1 + 32] = taps[:, N2 * n1 : N2 * n1 + N2]

    def filter_work(group, carry):
        forward = []
        for item in range(0, GROUP, 2):
            rows = [filters[pl.ds(group * GROUP + item + i, N1, stride=32)] for i in range(2)]
            high, low = split(jnp.concatenate(rows, axis=1))
            left = first_both[...]
            out = dot(left, jnp.concatenate([high, high], axis=0)) + dot(left[:, :N1], low)
            forward += [twisted(out[:, :N2], twist), twisted(out[:, N2:], twist)]
        rows = pl.ds(pl.multiple_of(group * GROUP * N1, GROUP * N1), GROUP * N1)
        filter_spectra[rows] = middle(jnp.concatenate(forward, axis=0), mats[0], mats[1])
        return carry

    lax.fori_loop(0, 2 * HALF // GROUP, filter_work, 0)

    for half in range(2):
        steps(lambda there: out_copy(half, there, there).wait_recv())
        own[half].wait()

        def unpack(n1, carry):
            rows = arrived[n1, half].reshape(32, N2).astype(F32)
            signals[pl.ds(pl.multiple_of(n1 * 32, 32), 32)] = rows
            return carry

        lax.fori_loop(0, N1, unpack, 0)

        def work(group, carry):
            forward = []
            for item in range(GROUP):
                rows = [signals[pl.ds(group * GROUP + item + HALF * i, N1, stride=32)] for i in range(2)]
                data = jnp.concatenate(rows, axis=1).astype(BF16)
                out = dot(first_both[...], jnp.concatenate([data, data], axis=0))
                forward += [twisted(out[:, :N2], twist), twisted(out[:, N2:], twist)]
            spectra[...] = middle(jnp.concatenate(forward, axis=0), mats[0], mats[1])
            inverse = []
            for item in range(GROUP):
                start = (half * HALF + group * GROUP + item) * N1
                h = filter_spectra[pl.ds(pl.multiple_of(start, N1), N1)]
                h_re, h_im = h[:, :N2], h[:, N2:]
                u = spectra[2 * item * N1 : (2 * item + 1) * N1]
                u_re, u_im = u[:, :N2], u[:, N2:]
                m = spectra[(2 * item + 1) * N1 : (2 * item + 2) * N1]
                m_re, m_im = m[:, :N2], m[:, N2:]
                inverse.append(jnp.concatenate([h_re * u_re - h_im * u_im, h_re * u_im + h_im * u_re], axis=1))
                inverse.append(jnp.concatenate([m_re * h_re + m_im * h_im, m_im * h_re - m_re * h_im], axis=1))
                inverse.append(jnp.concatenate([m_re * u_re + m_im * u_im, m_im * u_re - m_re * u_im], axis=1))
            results[...] = middle(jnp.concatenate(inverse, axis=0), mats[2], mats[3])

            def finish(indices):
                turned = [untwisted(results[N1 * i : N1 * i + N1], twist) for i in indices]
                high, low = split(jnp.concatenate(turned, axis=1))
                out = dot(last_all[...], jnp.concatenate([high, low, high], axis=0))
                return out[:, :N2], out[:, N2:]

            for item in range(GROUP):
                c = group * GROUP + item
                conv, inner = finish((3 * item, 3 * item + 1))
                signals[pl.ds(c, N1, stride=32)] = conv
                signals[pl.ds(c + HALF, N1, stride=32)] = inner
            for item in range(0, GROUP, 2):
                c = group * GROUP + item
                first, second = finish((3 * item + 2, 3 * item + 5))
                sums[half, pl.ds(c, N1, stride=HALF)] = first * scale
                sums[half, pl.ds(c + 1, N1, stride=HALF)] = second * scale
            return carry

        lax.fori_loop(0, HALF // GROUP, work, 0)

        def pack(n1, carry):
            rows = signals[pl.ds(pl.multiple_of(n1 * 32, 32), 32)].astype(BF16)
            back[n1, half] = rows.reshape(2, 16, N2)
            return carry

        lax.fori_loop(0, N1, pack, 0)
        for z in range(4):
            pair_copy(half, z).start()
        steps(lambda there: back_copy(half, there, ctx).start())
        keep[half].start()
        for z in range(4):
            pair_copy(half, z).wait()
            mine = sums[half, pl.ds(pl.multiple_of((z * 2 + core) * 64, 64), 64)]
            parts[half, z] = (mine + pair_sums[half, z]).astype(BF16).reshape(2, 2, HALF, N2)
        for away in (2, 1, 3):
            part_copy(half, (z_hi + away) % 4, z_hi).start()
        keep[2 + half].start()

    for copy in keep:
        copy.wait()
    for half in range(2):
        steps(lambda there: out_copy(half, there, there).wait_send())
        steps(lambda there: back_copy(half, there, there).wait())
        for away in (2, 1, 3):
            there = (z_hi + away) % 4
            part_copy(half, there, there).wait()


def gate_kernel(landed, query, key, value, grad, query_grad, key_grad, value_grad, taps_grad):
    for block in range(8):
        lanes = slice(128 * block, 128 * block + 128)
        devices = slice(4 * block, 4 * block + 4)
        conv = landed[devices, :, 0].reshape(128, N2).astype(F32).T
        inner = landed[devices, :, 1].reshape(128, N2).astype(F32).T
        query_grad[:, lanes] = (conv * grad[:, lanes].astype(F32)).astype(BF16)
        key_grad[:, lanes] = (inner * value[:, lanes].astype(F32)).astype(BF16)
        value_grad[:, lanes] = (inner * key[:, lanes].astype(F32)).astype(BF16)
    for half in range(2):
        total = landed[N1 + 4 * half].reshape(4 * HALF, N2).astype(F32)
        for z in range(1, 4):
            total = total + landed[N1 + 4 * half + z].reshape(4 * HALF, N2).astype(F32)
        for n1 in range(4):
            taps_grad[16 * half : 16 * half + 16, N2 * n1 : N2 * n1 + N2] = total[16 * n1 : 16 * n1 + 16]


def on_device(query_proj, key_proj, value_proj, out_grad, filter_taps):
    rows = query_proj.shape[1]
    query, key, value, grad = (a.reshape(rows, -1) for a in (query_proj, key_proj, value_proj, out_grad))
    vmem = pl.BlockSpec(memory_space=pltpu.VMEM)
    anywhere = pl.BlockSpec(memory_space=pl.ANY)
    limit = 62 * 1024 * 1024
    slabs = (N1, 2, 2, HALF, N2)
    scale = 1.0 / math.sqrt(lax.axis_size("dp") * LENGTH)
    dma = pltpu.SemaphoreType.DMA
    landed = pl.pallas_call(
        functools.partial(fused_kernel, scale),
        out_shape=jax.ShapeDtypeStruct((N1 + 8,) + slabs[1:], BF16),
        in_specs=[anywhere] * 9,
        out_specs=anywhere,
        scratch_shapes=[
            pltpu.VMEM((4, rows, query.shape[1]), BF16),
            pltpu.VMEM((2 * HALF, LENGTH), F32),
            pltpu.VMEM((2 * N1, 2 * N1), BF16),
            pltpu.VMEM((N1, 6 * N1), BF16),
            pltpu.VMEM((2, N1, N2), F32),
            pltpu.VMEM((4, 2 * N2, 2 * N2), BF16),
            pltpu.VMEM(slabs, BF16),
            pltpu.VMEM(slabs, BF16),
            pltpu.VMEM(slabs, BF16),
            pltpu.VMEM((N1 * 2 * HALF, N2), F32),
            pltpu.VMEM((N1 * 2 * HALF, N2), F32),
            pltpu.VMEM((2 * HALF * N1, 2 * N2), F32),
            pltpu.VMEM((2 * GROUP * N1, 2 * N2), F32),
            pltpu.VMEM((3 * GROUP * N1, 2 * N2), F32),
            pltpu.VMEM((2, N1 * HALF, N2), F32),
            pltpu.VMEM((2, 4, 64, N2), F32),
            pltpu.VMEM((2, 4, 2, 2, HALF, N2), BF16),
            dma((9,)),
            dma((2, 32)),
            dma((2, 32)),
            dma((2, 32)),
            dma((2, 32)),
            dma((6,)),
            dma((2, 4)),
            dma((2, 4)),
            dma((2, 4)),
            dma((2, 4)),
        ],
        compiler_params=pltpu.CompilerParams(collective_id=0, has_side_effects=True, vmem_limit_bytes=limit),
        name="exchange_convolve",
    )(query, key, value, grad, filter_taps.T, *(jnp.asarray(t) for t in tables()))
    flat = jax.ShapeDtypeStruct(query.shape, BF16)
    outs = pl.pallas_call(
        gate_kernel,
        out_shape=(flat, flat, flat, jax.ShapeDtypeStruct((2 * HALF, 4 * N2), F32)),
        in_specs=[vmem] * 5,
        out_specs=(vmem,) * 4,
        compiler_params=pltpu.CompilerParams(vmem_limit_bytes=48 * 1024 * 1024),
        name="gate",
    )(landed, query, key, value, grad)
    return tuple(o.reshape(query_proj.shape) for o in outs[:3]) + (outs[3].T,)


def solution(mesh):
    placed = (P("dp", "ctx", None),) * 4 + (P(None, "ctx"),)
    return jax.shard_map(
        on_device,
        mesh=mesh,
        in_specs=placed,
        out_specs=(P("dp", "ctx", None),) * 3 + (P("dp", "ctx"),),
        check_vma=False,
    )
```

```python
import functools
import math

import jax
import jax.numpy as jnp
import ml_dtypes
import numpy as np
from jax import lax
from jax.experimental import pallas as pl
from jax.experimental.pallas import tpu as pltpu
from jax.sharding import PartitionSpec as P

MESH = pl.DeviceIdType.MESH
F32 = jnp.float32
BF16 = jnp.bfloat16

N1 = 32
N2 = 128
LENGTH = N1 * N2
GROUP = 8
HALF = 16


def high_low(table):
    high = table.astype(ml_dtypes.bfloat16)
    low = (table - high.astype(np.float64)).astype(ml_dtypes.bfloat16)
    return high, low


@functools.lru_cache(maxsize=None)
def tables():
    row = np.arange(N1)
    col = np.arange(N2)
    outer = 2 * np.pi * np.outer(row + 0.25, row) / N1
    first = np.concatenate([np.cos(outer), -np.sin(outer)], axis=0)
    first_high, first_low = high_low(first)
    first_both = np.concatenate([first_high, first_low], axis=1)
    last = np.concatenate([np.cos(outer.T), -np.sin(outer.T)], axis=1) / LENGTH
    last_high, last_low = high_low(last)
    last_all = np.concatenate([last_high, last_high, last_low], axis=1)
    turn = 2 * np.pi * np.outer(row + 0.25, col) / LENGTH
    twist = np.stack([np.cos(turn), -np.sin(turn)]).astype(np.float32)
    inner = 2 * np.pi * (np.outer(col, col) % N2) / N2
    cos, sin = np.cos(inner), np.sin(inner)
    forward = np.block([[cos, -sin], [sin, cos]])
    inverse = np.block([[cos, sin], [-sin, cos]])
    stacked = []
    for matrix in (forward, inverse):
        high, low = high_low(matrix)
        stacked.append(np.concatenate([high, high, low], axis=0))
    stacked = np.stack(stacked)
    return first_both, last_all, twist, stacked


def place():
    dp = lax.axis_index("dp")
    ctx = lax.axis_index("ctx")
    return dp // 2, dp % 2, ctx


OFFSETS = sorted(
    ((dx, dz, dy) for dx in range(4) for dz in range(2) for dy in range(4) if dx or dz or dy),
    key=lambda o: -(min(o[0], 4 - o[0]) + o[1] + min(o[2], 4 - o[2])),
)


def split(value):
    high = value.astype(BF16)
    return high, (value - high.astype(F32)).astype(BF16)


def dot(left, right):
    return lax.dot_general(left, right, (((1,), (0,)), ((), ())), preferred_element_type=F32)


def middle(value, stacked):
    high, low = split(value)
    return dot(jnp.concatenate([high, low, high], axis=1), stacked[...])


def twisted(value, twist):
    re, im = value[:N1], value[N1:]
    return jnp.concatenate([re * twist[0] - im * twist[1], re * twist[1] + im * twist[0]], axis=1)


def untwisted(value, twist):
    re, im = value[:, :N2], value[:, N2:]
    return jnp.concatenate([re * twist[0] + im * twist[1], im * twist[0] - re * twist[1]], axis=0)


def fused_kernel(
    scale, query_hbm, key_hbm, value_hbm, grad_hbm, taps_hbm, first_hbm, last_hbm, twist_hbm, mats_hbm, landed,
    inputs, taps, first_both, last_all, twist_ref, mats, packed, arrived, back, signals, filters, filter_spectra, spectra, results, sums, pair_sums, parts,
    load_sem, out_send, out_recv, back_send, back_recv, own_sem, pair_send, pair_recv, part_send, part_recv,
):
    z_hi, core, ctx = place()
    dp = z_hi * 2 + core
    pair = (z_hi * 2 + (core + 1) % 2, ctx)
    loads = [
        pltpu.make_async_copy(ref, inputs.at[i], load_sem.at[i])
        for i, ref in enumerate((key_hbm, value_hbm, grad_hbm, query_hbm))
    ]
    later = ((taps_hbm, taps), (first_hbm, first_both), (last_hbm, last_all), (twist_hbm, twist_ref), (mats_hbm, mats))
    loads += [pltpu.make_async_copy(ref, held, load_sem.at[4 + i]) for i, (ref, held) in enumerate(later)]
    for load in loads:
        load.start()

    barrier = pltpu.get_barrier_semaphore()

    xs = [((ctx // 8 + d) % 4) * 8 for d in range(4)]
    zs = [((ctx // 4 + d) % 2) * 4 for d in range(2)]
    ys = [(ctx + d) % 4 for d in range(4)]
    partners = [xs[dx] + zs[dz] + ys[dy] for dx, dz, dy in OFFSETS]
    for there in partners:
        pl.semaphore_signal(barrier, inc=1, device_id=(dp, there), device_id_type=MESH)
    pl.semaphore_signal(barrier, inc=1, device_id=pair, device_id_type=MESH)
    for away in range(1, 4):
        there = ((z_hi + away) % 4) * 2 + core
        pl.semaphore_signal(barrier, inc=1, device_id=(there, ctx), device_id_type=MESH)

    def out_copy(half, there):
        return pltpu.make_async_remote_copy(
            src_ref=packed.at[half, there],
            dst_ref=arrived.at[half, ctx],
            send_sem=out_send.at[half],
            recv_sem=out_recv.at[half],
            device_id=(dp, there),
            device_id_type=MESH,
        )

    def back_copy(half, there):
        return pltpu.make_async_remote_copy(
            src_ref=back.at[half, there],
            dst_ref=landed.at[half * N1 + ctx],
            send_sem=back_send.at[half],
            recv_sem=back_recv.at[half],
            device_id=(dp, there),
            device_id_type=MESH,
        )

    def wait_for(ref, sem):
        pltpu.make_async_copy(ref, ref, sem).wait()

    def pair_copy(half, z):
        return pltpu.make_async_remote_copy(
            src_ref=sums.at[half, pl.ds((z * 2 + (core + 1) % 2) * 64, 64)],
            dst_ref=pair_sums.at[half, z],
            send_sem=pair_send.at[half, z],
            recv_sem=pair_recv.at[half, z],
            device_id=pair,
            device_id_type=MESH,
        )

    def part_copy(half, there, slot):
        return pltpu.make_async_remote_copy(
            src_ref=parts.at[half, there],
            dst_ref=landed.at[pl.ds(2 * N1 + (half * 4 + slot) * 2, 2)],
            send_sem=part_send.at[half, there],
            recv_sem=part_recv.at[half, slot],
            device_id=(there * 2 + core, ctx),
            device_id_type=MESH,
        )

    for load in loads[:4]:
        load.wait()
    for order, (dx, dz) in enumerate(((2, 1), (2, 0), (1, 1), (3, 1), (1, 0), (3, 0), (0, 1), (0, 0))):
        first = xs[dx] + zs[dz]
        lanes = pl.ds(pl.multiple_of(first * 32, 128), 128)
        for array in range(2):
            gated = inputs[2 * array, :, lanes].astype(F32) * inputs[2 * array + 1, :, lanes].astype(F32)
            turned = gated.T.astype(BF16)
            for part in range(8):
                packed[part % 2, first + part // 2, array] = turned[16 * part : 16 * part + 16]
        if order == 0:
            pl.semaphore_wait(barrier, 35)
        for dy in (2, 1, 3, 0):
            if dx or dz or dy:
                out_copy(0, first + ys[dy]).start()
    own = [
        pltpu.make_async_copy(packed.at[half, ctx], arrived.at[half, ctx], out_recv.at[half]) for half in range(2)
    ]
    keep = [
        pltpu.make_async_copy(back.at[half, ctx], landed.at[half * N1 + ctx], back_recv.at[half]) for half in range(2)
    ] + [
        pltpu.make_async_copy(
            parts.at[half, z_hi], landed.at[pl.ds(2 * N1 + (half * 4 + z_hi) * 2, 2)], own_sem.at[half]
        )
        for half in range(2)
    ]
    own[0].start()
    own[1].start()
    for there in partners:
        out_copy(1, there).start()

    for load in loads[4:]:
        load.wait()
    twist = (twist_ref[0], twist_ref[1])
    for n1 in range(N1):
        filters[32 * n1 : 32 * n1 + 32] = taps[:, N2 * n1 : N2 * n1 + N2]

    def filter_work(group, carry):
        forward = []
        for item in range(0, GROUP, 2):
            rows = [filters[pl.ds(group * GROUP + item + i, N1, stride=32)] for i in range(2)]
            high, low = split(jnp.concatenate(rows, axis=1))
            left = first_both[...]
            out = dot(left, jnp.concatenate([high, high], axis=0)) + dot(left[:, :N1], low)
            forward += [twisted(out[:, :N2], twist), twisted(out[:, N2:], twist)]
        rows = pl.ds(pl.multiple_of(group * GROUP * N1, GROUP * N1), GROUP * N1)
        filter_spectra[rows] = middle(jnp.concatenate(forward, axis=0), mats.at[0])
        return carry

    lax.fori_loop(0, 2 * HALF // GROUP, filter_work, 0)

    for half in range(2):
        wait_for(arrived.at[half], out_recv.at[half])

        def unpack(n1, carry):
            rows = arrived[half, n1].reshape(32, N2).astype(F32)
            signals[pl.ds(pl.multiple_of(n1 * 32, 32), 32)] = rows
            return carry

        lax.fori_loop(0, N1, unpack, 0, unroll=8)

        def work(group, carry):
            forward = []
            for item in range(GROUP):
                rows = [signals[pl.ds(group * GROUP + item + HALF * i, N1, stride=32)] for i in range(2)]
                data = jnp.concatenate(rows, axis=1).astype(BF16)
                out = dot(first_both[...], jnp.concatenate([data, data], axis=0))
                forward += [twisted(out[:, :N2], twist), twisted(out[:, N2:], twist)]
            spectra[...] = middle(jnp.concatenate(forward, axis=0), mats.at[0])
            inverse = []
            for item in range(GROUP):
                start = (half * HALF + group * GROUP + item) * N1
                h = filter_spectra[pl.ds(pl.multiple_of(start, N1), N1)]
                h_re, h_im = h[:, :N2], h[:, N2:]
                u = spectra[2 * item * N1 : (2 * item + 1) * N1]
                u_re, u_im = u[:, :N2], u[:, N2:]
                m = spectra[(2 * item + 1) * N1 : (2 * item + 2) * N1]
                m_re, m_im = m[:, :N2], m[:, N2:]
                inverse.append(jnp.concatenate([h_re * u_re - h_im * u_im, h_re * u_im + h_im * u_re], axis=1))
                inverse.append(jnp.concatenate([m_re * h_re + m_im * h_im, m_im * h_re - m_re * h_im], axis=1))
                inverse.append(jnp.concatenate([m_re * u_re + m_im * u_im, m_im * u_re - m_re * u_im], axis=1))
            results[...] = middle(jnp.concatenate(inverse, axis=0), mats.at[1])

            def finish(indices):
                turned = [untwisted(results[N1 * i : N1 * i + N1], twist) for i in indices]
                high, low = split(jnp.concatenate(turned, axis=1))
                out = dot(last_all[...], jnp.concatenate([high, low, high], axis=0))
                return out[:, :N2], out[:, N2:]

            for item in range(0, GROUP, 2):
                c = group * GROUP + item
                first, second = finish((3 * item + 2, 3 * item + 5))
                sums[half, pl.ds(c, N1, stride=HALF)] = first * scale
                sums[half, pl.ds(c + 1, N1, stride=HALF)] = second * scale

            @pl.when(group == HALF // GROUP - 1)
            def _():
                for z in range(4):
                    pair_copy(half, z).start()

            for item in range(GROUP):
                c = group * GROUP + item
                conv, inner = finish((3 * item, 3 * item + 1))
                signals[pl.ds(c, N1, stride=32)] = conv
                signals[pl.ds(c + HALF, N1, stride=32)] = inner
            return carry

        lax.fori_loop(0, HALF // GROUP, work, 0)

        def pack(n1, carry):
            rows = signals[pl.ds(pl.multiple_of(n1 * 32, 32), 32)].astype(BF16)
            back[half, n1] = rows.reshape(2, 16, N2)
            return carry

        lax.fori_loop(0, N1, pack, 0, unroll=8)
        for there in partners:
            back_copy(half, there).start()
        keep[half].start()
        for z in range(4):
            pair_copy(half, z).wait()
            mine = sums[half, pl.ds(pl.multiple_of((z * 2 + core) * 64, 64), 64)]
            parts[half, z] = (mine + pair_sums[half, z]).astype(BF16).reshape(2, 2, HALF, N2)
        for away in (2, 1, 3):
            part_copy(half, (z_hi + away) % 4, z_hi).start()
        keep[2 + half].start()

    for half in range(2):
        wait_for(packed.at[half, pl.ds(0, N1 - 1)], out_send.at[half])
        wait_for(back.at[half, pl.ds(0, N1 - 1)], back_send.at[half])
        wait_for(landed.at[pl.ds(half * N1, N1)], back_recv.at[half])
        keep[2 + half].wait()
        for away in (2, 1, 3):
            there = (z_hi + away) % 4
            part_copy(half, there, there).wait()


def gate_kernel(landed, query, key, value, grad, query_grad, key_grad, value_grad, taps_grad):
    for block in range(8):
        lanes = slice(128 * block, 128 * block + 128)
        slots = [half * N1 + 4 * block + device for device in range(4) for half in range(2)]
        conv = jnp.concatenate([landed[slot, 0] for slot in slots], axis=0).astype(F32).T
        inner = jnp.concatenate([landed[slot, 1] for slot in slots], axis=0).astype(F32).T
        query_grad[:, lanes] = (conv * grad[:, lanes].astype(F32)).astype(BF16)
        key_grad[:, lanes] = (inner * value[:, lanes].astype(F32)).astype(BF16)
        value_grad[:, lanes] = (inner * key[:, lanes].astype(F32)).astype(BF16)
    for half in range(2):
        pieces = [2 * N1 + (4 * half + z) * 2 for z in range(4)]
        total = landed[pieces[0] : pieces[0] + 2].reshape(4 * HALF, N2).astype(F32)
        for piece in pieces[1:]:
            total = total + landed[piece : piece + 2].reshape(4 * HALF, N2).astype(F32)
        for n1 in range(4):
            taps_grad[16 * half : 16 * half + 16, N2 * n1 : N2 * n1 + N2] = total[16 * n1 : 16 * n1 + 16]


def on_device(query_proj, key_proj, value_proj, out_grad, filter_taps):
    rows = query_proj.shape[1]
    query, key, value, grad = (a.reshape(rows, -1) for a in (query_proj, key_proj, value_proj, out_grad))
    vmem = pl.BlockSpec(memory_space=pltpu.VMEM)
    anywhere = pl.BlockSpec(memory_space=pl.ANY)
    limit = 62 * 1024 * 1024
    slabs = (2, N1, 2, HALF, N2)
    scale = 1.0 / math.sqrt(lax.axis_size("dp") * LENGTH)
    dma = pltpu.SemaphoreType.DMA
    landed = pl.pallas_call(
        functools.partial(fused_kernel, scale),
        out_shape=jax.ShapeDtypeStruct((2 * N1 + 16, 2, HALF, N2), BF16),
        in_specs=[anywhere] * 9,
        out_specs=anywhere,
        scratch_shapes=[
            pltpu.VMEM((4, rows, query.shape[1]), BF16),
            pltpu.VMEM((2 * HALF, LENGTH), F32),
            pltpu.VMEM((2 * N1, 2 * N1), BF16),
            pltpu.VMEM((N1, 6 * N1), BF16),
            pltpu.VMEM((2, N1, N2), F32),
            pltpu.VMEM((2, 6 * N2, 2 * N2), BF16),
            pltpu.VMEM(slabs, BF16),
            pltpu.VMEM(slabs, BF16),
            pltpu.VMEM(slabs, BF16),
            pltpu.VMEM((N1 * 2 * HALF, N2), F32),
            pltpu.VMEM((N1 * 2 * HALF, N2), F32),
            pltpu.VMEM((2 * HALF * N1, 2 * N2), F32),
            pltpu.VMEM((2 * GROUP * N1, 2 * N2), F32),
            pltpu.VMEM((3 * GROUP * N1, 2 * N2), F32),
            pltpu.VMEM((2, N1 * HALF, N2), F32),
            pltpu.VMEM((2, 4, 64, N2), F32),
            pltpu.VMEM((2, 4, 2, 2, HALF, N2), BF16),
            dma((9,)),
            dma((2,)),
            dma((2,)),
            dma((2,)),
            dma((2,)),
            dma((2,)),
            dma((2, 4)),
            dma((2, 4)),
            dma((2, 4)),
            dma((2, 4)),
        ],
        compiler_params=pltpu.CompilerParams(collective_id=0, has_side_effects=True, vmem_limit_bytes=limit),
        name="exchange_convolve",
    )(query, key, value, grad, filter_taps.T, *(jnp.asarray(t) for t in tables()))
    flat = jax.ShapeDtypeStruct(query.shape, BF16)
    outs = pl.pallas_call(
        gate_kernel,
        out_shape=(flat, flat, flat, jax.ShapeDtypeStruct((2 * HALF, 4 * N2), F32)),
        in_specs=[vmem] * 5,
        out_specs=(vmem,) * 4,
        compiler_params=pltpu.CompilerParams(vmem_limit_bytes=48 * 1024 * 1024),
        name="gate",
    )(landed, query, key, value, grad)
    return tuple(o.reshape(query_proj.shape) for o in outs[:3]) + (outs[3].T,)


def solution(mesh):
    placed = (P("dp", "ctx", None),) * 4 + (P(None, "ctx"),)
    return jax.shard_map(
        on_device,
        mesh=mesh,
        in_specs=placed,
        out_specs=(P("dp", "ctx", None),) * 3 + (P("dp", "ctx"),),
        check_vma=False,
    )
```

```python
import functools
import math

import jax
import jax.numpy as jnp
import ml_dtypes
import numpy as np
from jax import lax
from jax.experimental import pallas as pl
from jax.experimental.pallas import tpu as pltpu
from jax.sharding import PartitionSpec as P

MESH = pl.DeviceIdType.MESH
F32 = jnp.float32
BF16 = jnp.bfloat16

N1 = 32
N2 = 128
LENGTH = N1 * N2
GROUP = 8
HALF = 16


def high_low(table):
    high = table.astype(ml_dtypes.bfloat16)
    low = (table - high.astype(np.float64)).astype(ml_dtypes.bfloat16)
    return high, low


@functools.lru_cache(maxsize=None)
def tables():
    row = np.arange(N1)
    col = np.arange(N2)
    outer = 2 * np.pi * np.outer(row + 0.25, row) / N1
    first = np.concatenate([np.cos(outer), -np.sin(outer)], axis=0)
    first_high, first_low = high_low(first)
    first_both = np.concatenate([first_high, first_low], axis=1)
    last = np.concatenate([np.cos(outer.T), -np.sin(outer.T)], axis=1) / LENGTH
    last_high, last_low = high_low(last)
    last_all = np.concatenate([last_high, last_high, last_low], axis=1)
    turn = 2 * np.pi * np.outer(row + 0.25, col) / LENGTH
    twist = np.stack([np.cos(turn), -np.sin(turn)]).astype(np.float32)
    inner = 2 * np.pi * (np.outer(col, col) % N2) / N2
    cos, sin = np.cos(inner), np.sin(inner)
    forward = np.block([[cos, -sin], [sin, cos]])
    inverse = np.block([[cos, sin], [-sin, cos]])
    stacked = []
    for matrix in (forward, inverse):
        high, low = high_low(matrix)
        stacked.append(np.concatenate([high, high, low], axis=0))
    stacked = np.stack(stacked)
    return first_both, last_all, twist, stacked


def place():
    dp = lax.axis_index("dp")
    ctx = lax.axis_index("ctx")
    return dp // 2, dp % 2, ctx


OFFSETS = sorted(
    ((dx, dz, dy) for dx in range(4) for dz in range(2) for dy in range(4) if dx or dz or dy),
    key=lambda o: -(min(o[0], 4 - o[0]) + o[1] + min(o[2], 4 - o[2])),
)


def split(value):
    high = value.astype(BF16)
    return high, (value - high.astype(F32)).astype(BF16)


def dot(left, right):
    return lax.dot_general(left, right, (((1,), (0,)), ((), ())), preferred_element_type=F32)


def middle(value, stacked):
    high, low = split(value)
    return dot(jnp.concatenate([high, low, high], axis=1), stacked[...])


def twisted(value, twist):
    re, im = value[:N1], value[N1:]
    return jnp.concatenate([re * twist[0] - im * twist[1], re * twist[1] + im * twist[0]], axis=1)


def untwisted(value, twist):
    re, im = value[:, :N2], value[:, N2:]
    return jnp.concatenate([re * twist[0] + im * twist[1], im * twist[0] - re * twist[1]], axis=0)


def fused_kernel(
    scale, query_hbm, key_hbm, value_hbm, grad_hbm, taps_hbm, first_hbm, last_hbm, twist_hbm, mats_hbm, landed,
    inputs, taps, first_both, last_all, twist_ref, mats, packed, arrived, back, signals, filters, filter_spectra, spectra, results, sums, pair_sums, parts,
    load_sem, out_send, out_recv, back_send, back_recv, own_sem, pair_send, pair_recv, part_send, part_recv,
):
    z_hi, core, ctx = place()
    dp = z_hi * 2 + core
    pair = (z_hi * 2 + (core + 1) % 2, ctx)
    loads = [
        pltpu.make_async_copy(ref, inputs.at[i], load_sem.at[i])
        for i, ref in enumerate((key_hbm, value_hbm, grad_hbm, query_hbm))
    ]
    later = ((taps_hbm, taps), (first_hbm, first_both), (last_hbm, last_all), (twist_hbm, twist_ref), (mats_hbm, mats))
    loads += [pltpu.make_async_copy(ref, held, load_sem.at[4 + i]) for i, (ref, held) in enumerate(later)]
    for load in loads:
        load.start()

    barrier = pltpu.get_barrier_semaphore()

    xs = [((ctx // 8 + d) % 4) * 8 for d in range(4)]
    zs = [((ctx // 4 + d) % 2) * 4 for d in range(2)]
    ys = [(ctx + d) % 4 for d in range(4)]
    partners = [xs[dx] + zs[dz] + ys[dy] for dx, dz, dy in OFFSETS]
    for there in partners:
        pl.semaphore_signal(barrier, inc=1, device_id=(dp, there), device_id_type=MESH)
    pl.semaphore_signal(barrier, inc=1, device_id=pair, device_id_type=MESH)
    for away in range(1, 4):
        there = ((z_hi + away) % 4) * 2 + core
        pl.semaphore_signal(barrier, inc=1, device_id=(there, ctx), device_id_type=MESH)

    def out_copy(half, there):
        return pltpu.make_async_remote_copy(
            src_ref=packed.at[half, there],
            dst_ref=arrived.at[half, ctx],
            send_sem=out_send.at[half],
            recv_sem=out_recv.at[half],
            device_id=(dp, there),
            device_id_type=MESH,
        )

    def back_copy(half, there):
        return pltpu.make_async_remote_copy(
            src_ref=back.at[half, there],
            dst_ref=landed.at[half * N1 + ctx],
            send_sem=back_send.at[half],
            recv_sem=back_recv.at[half],
            device_id=(dp, there),
            device_id_type=MESH,
        )

    def wait_for(ref, sem):
        pltpu.make_async_copy(ref, ref, sem).wait()

    def pair_copy(half, z):
        return pltpu.make_async_remote_copy(
            src_ref=sums.at[half, pl.ds((z * 2 + (core + 1) % 2) * 64, 64)],
            dst_ref=pair_sums.at[half, z],
            send_sem=pair_send.at[half, z],
            recv_sem=pair_recv.at[half, z],
            device_id=pair,
            device_id_type=MESH,
        )

    def part_copy(half, there, slot):
        return pltpu.make_async_remote_copy(
            src_ref=parts.at[half, there],
            dst_ref=landed.at[pl.ds(2 * N1 + (half * 4 + slot) * 2, 2)],
            send_sem=part_send.at[half, there],
            recv_sem=part_recv.at[half, slot],
            device_id=(there * 2 + core, ctx),
            device_id_type=MESH,
        )

    for load in loads[:4]:
        load.wait()
    for order, (dx, dz) in enumerate(((2, 1), (2, 0), (1, 1), (3, 1), (1, 0), (3, 0), (0, 1), (0, 0))):
        first = xs[dx] + zs[dz]
        lanes = pl.ds(pl.multiple_of(first * 32, 128), 128)
        for array in range(2):
            gated = inputs[2 * array, :, lanes].astype(F32) * inputs[2 * array + 1, :, lanes].astype(F32)
            turned = gated.astype(BF16).T
            for part in range(8):
                packed[part % 2, first + part // 2, array] = turned[16 * part : 16 * part + 16]
        if order == 0:
            pl.semaphore_wait(barrier, 35)
        for dy in (2, 1, 3, 0):
            if dx or dz or dy:
                out_copy(0, first + ys[dy]).start()
    own = [
        pltpu.make_async_copy(packed.at[half, ctx], arrived.at[half, ctx], out_recv.at[half]) for half in range(2)
    ]
    keep = [
        pltpu.make_async_copy(back.at[half, ctx], landed.at[half * N1 + ctx], back_recv.at[half]) for half in range(2)
    ] + [
        pltpu.make_async_copy(
            parts.at[half, z_hi], landed.at[pl.ds(2 * N1 + (half * 4 + z_hi) * 2, 2)], own_sem.at[half]
        )
        for half in range(2)
    ]
    own[0].start()
    own[1].start()
    for there in partners:
        out_copy(1, there).start()

    for load in loads[4:]:
        load.wait()
    twist = (twist_ref[0], twist_ref[1])
    for n1 in range(N1):
        filters[32 * n1 : 32 * n1 + 32] = taps[:, N2 * n1 : N2 * n1 + N2]

    def filter_work(group, carry):
        forward = []
        for item in range(0, GROUP, 2):
            rows = [filters[pl.ds(group * GROUP + item + i, N1, stride=32)] for i in range(2)]
            high, low = split(jnp.concatenate(rows, axis=1))
            left = first_both[...]
            out = dot(left, jnp.concatenate([high, high], axis=0)) + dot(left[:, :N1], low)
            forward += [twisted(out[:, :N2], twist), twisted(out[:, N2:], twist)]
        rows = pl.ds(pl.multiple_of(group * GROUP * N1, GROUP * N1), GROUP * N1)
        filter_spectra[rows] = middle(jnp.concatenate(forward, axis=0), mats.at[0])
        return carry

    lax.fori_loop(0, 2 * HALF // GROUP, filter_work, 0)

    def sum_parts(half):
        for z in range(4):
            pair_copy(half, z).wait()
            mine = sums[half, pl.ds(pl.multiple_of((z * 2 + core) * 64, 64), 64)]
            parts[half, z] = (mine + pair_sums[half, z]).astype(BF16).reshape(2, 2, HALF, N2)
        for away in (2, 1, 3):
            part_copy(half, (z_hi + away) % 4, z_hi).start()
        keep[2 + half].start()

    for half in range(2):
        wait_for(arrived.at[half], out_recv.at[half])

        def unpack(n1, carry):
            rows = arrived[half, n1].reshape(32, N2).astype(F32)
            signals[pl.ds(pl.multiple_of(n1 * 32, 32), 32)] = rows
            return carry

        lax.fori_loop(0, N1, unpack, 0, unroll=8)

        def spectrum(index):
            block = spectra[pl.ds(pl.multiple_of(index * N1, N1), N1)]
            return block[:, :N2], block[:, N2:]

        def finish(indices):
            turned = [untwisted(results[N1 * i : N1 * i + N1], twist) for i in indices]
            high, low = split(jnp.concatenate(turned, axis=1))
            out = dot(last_all[...], jnp.concatenate([high, low, high], axis=0))
            return out[:, :N2], out[:, N2:]

        def taps_work(group, carry):
            forward = []
            for item in range(GROUP):
                rows = [signals[pl.ds(group * GROUP + item + HALF * i, N1, stride=32)] for i in range(2)]
                data = jnp.concatenate(rows, axis=1).astype(BF16)
                out = dot(first_both[...], jnp.concatenate([data, data], axis=0))
                forward += [twisted(out[:, :N2], twist), twisted(out[:, N2:], twist)]
            rows = pl.ds(pl.multiple_of(group * 2 * GROUP * N1, 2 * GROUP * N1), 2 * GROUP * N1)
            spectra[rows] = middle(jnp.concatenate(forward, axis=0), mats.at[0])
            inverse = []
            for item in range(GROUP):
                u_re, u_im = spectrum(2 * (group * GROUP + item))
                m_re, m_im = spectrum(2 * (group * GROUP + item) + 1)
                inverse.append(jnp.concatenate([m_re * u_re + m_im * u_im, m_im * u_re - m_re * u_im], axis=1))
            results[: GROUP * N1] = middle(jnp.concatenate(inverse, axis=0), mats.at[1])
            for item in range(0, GROUP, 2):
                c = group * GROUP + item
                first, second = finish((item, item + 1))
                sums[half, pl.ds(c, N1, stride=HALF)] = first * scale
                sums[half, pl.ds(c + 1, N1, stride=HALF)] = second * scale
            return carry

        lax.fori_loop(0, HALF // GROUP, taps_work, 0)
        for z in range(4):
            pair_copy(half, z).start()
        if half == 1:
            sum_parts(0)

        def work(group, carry):
            inverse = []
            for item in range(GROUP):
                start = (half * HALF + group * GROUP + item) * N1
                h = filter_spectra[pl.ds(pl.multiple_of(start, N1), N1)]
                h_re, h_im = h[:, :N2], h[:, N2:]
                u_re, u_im = spectrum(2 * (group * GROUP + item))
                m_re, m_im = spectrum(2 * (group * GROUP + item) + 1)
                inverse.append(jnp.concatenate([h_re * u_re - h_im * u_im, h_re * u_im + h_im * u_re], axis=1))
                inverse.append(jnp.concatenate([m_re * h_re + m_im * h_im, m_im * h_re - m_re * h_im], axis=1))
            results[...] = middle(jnp.concatenate(inverse, axis=0), mats.at[1])
            for item in range(GROUP):
                c = group * GROUP + item
                conv, inner = finish((2 * item, 2 * item + 1))
                signals[pl.ds(c, N1, stride=32)] = conv
                signals[pl.ds(c + HALF, N1, stride=32)] = inner
            return carry

        lax.fori_loop(0, HALF // GROUP, work, 0)

        def pack(n1, carry):
            rows = signals[pl.ds(pl.multiple_of(n1 * 32, 32), 32)].astype(BF16)
            back[half, n1] = rows.reshape(2, 16, N2)
            return carry

        lax.fori_loop(0, N1, pack, 0, unroll=8)
        if half == 1:
            sum_parts(half)
        for there in partners:
            back_copy(half, there).start()
        keep[half].start()

    for half in range(2):
        wait_for(packed.at[half, pl.ds(0, N1 - 1)], out_send.at[half])
        wait_for(back.at[half, pl.ds(0, N1 - 1)], back_send.at[half])
        wait_for(landed.at[pl.ds(half * N1, N1)], back_recv.at[half])
        keep[2 + half].wait()
        for away in (2, 1, 3):
            there = (z_hi + away) % 4
            part_copy(half, there, there).wait()


def gate_kernel(landed, query, key, value, grad, query_grad, key_grad, value_grad, taps_grad):
    for block in range(8):
        lanes = slice(128 * block, 128 * block + 128)
        slots = [half * N1 + 4 * block + device for device in range(4) for half in range(2)]
        conv = jnp.concatenate([landed[slot, 0] for slot in slots], axis=0).astype(F32).T
        inner = jnp.concatenate([landed[slot, 1] for slot in slots], axis=0).astype(F32).T
        query_grad[:, lanes] = (conv * grad[:, lanes].astype(F32)).astype(BF16)
        key_grad[:, lanes] = (inner * value[:, lanes].astype(F32)).astype(BF16)
        value_grad[:, lanes] = (inner * key[:, lanes].astype(F32)).astype(BF16)
    for half in range(2):
        pieces = [2 * N1 + (4 * half + z) * 2 for z in range(4)]
        total = landed[pieces[0] : pieces[0] + 2].reshape(4 * HALF, N2).astype(F32)
        for piece in pieces[1:]:
            total = total + landed[piece : piece + 2].reshape(4 * HALF, N2).astype(F32)
        for n1 in range(4):
            taps_grad[16 * half : 16 * half + 16, N2 * n1 : N2 * n1 + N2] = total[16 * n1 : 16 * n1 + 16]


def on_device(query_proj, key_proj, value_proj, out_grad, filter_taps):
    rows = query_proj.shape[1]
    query, key, value, grad = (a.reshape(rows, -1) for a in (query_proj, key_proj, value_proj, out_grad))
    vmem = pl.BlockSpec(memory_space=pltpu.VMEM)
    anywhere = pl.BlockSpec(memory_space=pl.ANY)
    limit = 62 * 1024 * 1024
    slabs = (2, N1, 2, HALF, N2)
    scale = 1.0 / math.sqrt(lax.axis_size("dp") * LENGTH)
    dma = pltpu.SemaphoreType.DMA
    landed = pl.pallas_call(
        functools.partial(fused_kernel, scale),
        out_shape=jax.ShapeDtypeStruct((2 * N1 + 16, 2, HALF, N2), BF16),
        in_specs=[anywhere] * 9,
        out_specs=anywhere,
        scratch_shapes=[
            pltpu.VMEM((4, rows, query.shape[1]), BF16),
            pltpu.VMEM((2 * HALF, LENGTH), F32),
            pltpu.VMEM((2 * N1, 2 * N1), BF16),
            pltpu.VMEM((N1, 6 * N1), BF16),
            pltpu.VMEM((2, N1, N2), F32),
            pltpu.VMEM((2, 6 * N2, 2 * N2), BF16),
            pltpu.VMEM(slabs, BF16),
            pltpu.VMEM(slabs, BF16),
            pltpu.VMEM(slabs, BF16),
            pltpu.VMEM((N1 * 2 * HALF, N2), F32),
            pltpu.VMEM((N1 * 2 * HALF, N2), F32),
            pltpu.VMEM((2 * HALF * N1, 2 * N2), F32),
            pltpu.VMEM((2 * HALF * N1, 2 * N2), F32),
            pltpu.VMEM((2 * GROUP * N1, 2 * N2), F32),
            pltpu.VMEM((2, N1 * HALF, N2), F32),
            pltpu.VMEM((2, 4, 64, N2), F32),
            pltpu.VMEM((2, 4, 2, 2, HALF, N2), BF16),
            dma((9,)),
            dma((2,)),
            dma((2,)),
            dma((2,)),
            dma((2,)),
            dma((2,)),
            dma((2, 4)),
            dma((2, 4)),
            dma((2, 4)),
            dma((2, 4)),
        ],
        compiler_params=pltpu.CompilerParams(collective_id=0, has_side_effects=True, vmem_limit_bytes=limit),
        name="exchange_convolve",
    )(query, key, value, grad, filter_taps.T, *(jnp.asarray(t) for t in tables()))
    flat = jax.ShapeDtypeStruct(query.shape, BF16)
    outs = pl.pallas_call(
        gate_kernel,
        out_shape=(flat, flat, flat, jax.ShapeDtypeStruct((2 * HALF, 4 * N2), F32)),
        in_specs=[vmem] * 5,
        out_specs=(vmem,) * 4,
        compiler_params=pltpu.CompilerParams(vmem_limit_bytes=48 * 1024 * 1024),
        name="gate",
    )(landed, query, key, value, grad)
    return tuple(o.reshape(query_proj.shape) for o in outs[:3]) + (outs[3].T,)


def solution(mesh):
    placed = (P("dp", "ctx", None),) * 4 + (P(None, "ctx"),)
    return jax.shard_map(
        on_device,
        mesh=mesh,
        in_specs=placed,
        out_specs=(P("dp", "ctx", None),) * 3 + (P("dp", "ctx"),),
        check_vma=False,
    )
```

```python
import functools
import math

import jax
import jax.numpy as jnp
import ml_dtypes
import numpy as np
from jax import lax
from jax.experimental import pallas as pl
from jax.experimental.pallas import tpu as pltpu
from jax.sharding import PartitionSpec as P

MESH = pl.DeviceIdType.MESH
F32 = jnp.float32
BF16 = jnp.bfloat16

N1 = 32
N2 = 128
LENGTH = N1 * N2
GROUP = 16
HALF = 16


def high_low(table):
    high = table.astype(ml_dtypes.bfloat16)
    low = (table - high.astype(np.float64)).astype(ml_dtypes.bfloat16)
    return high, low


@functools.lru_cache(maxsize=None)
def tables():
    row = np.arange(N1)
    col = np.arange(N2)
    outer = 2 * np.pi * np.outer(row + 0.25, row) / N1
    first = np.concatenate([np.cos(outer), -np.sin(outer)], axis=0)
    first_high, first_low = high_low(first)
    first_both = np.concatenate([first_high, first_low], axis=1)
    last = np.concatenate([np.cos(outer.T), -np.sin(outer.T)], axis=1) / LENGTH
    last_high, last_low = high_low(last)
    last_all = np.concatenate([last_high, last_high, last_low], axis=1)
    turn = 2 * np.pi * np.outer(row + 0.25, col) / LENGTH
    twist = np.stack([np.cos(turn), -np.sin(turn)]).astype(np.float32)
    inner = 2 * np.pi * (np.outer(col, col) % N2) / N2
    cos, sin = np.cos(inner), np.sin(inner)
    forward = np.block([[cos, -sin], [sin, cos]])
    inverse = np.block([[cos, sin], [-sin, cos]])
    stacked = []
    for matrix in (forward, inverse):
        high, low = high_low(matrix)
        stacked.append(np.concatenate([high, high, low], axis=0))
    stacked = np.stack(stacked)
    return first_both, last_all, twist, stacked


def place():
    dp = lax.axis_index("dp")
    ctx = lax.axis_index("ctx")
    return dp // 2, dp % 2, ctx


OFFSETS = sorted(
    ((dx, dz, dy) for dx in range(4) for dz in range(2) for dy in range(4) if dx or dz or dy),
    key=lambda o: -(min(o[0], 4 - o[0]) + o[1] + min(o[2], 4 - o[2])),
)


def split(value):
    high = value.astype(BF16)
    return high, (value - high.astype(F32)).astype(BF16)


def dot(left, right):
    return lax.dot_general(left, right, (((1,), (0,)), ((), ())), preferred_element_type=F32)


def middle(value, stacked):
    high, low = split(value)
    return dot(jnp.concatenate([high, low, high], axis=1), stacked[...])


def twisted(value, twist):
    re, im = value[:N1], value[N1:]
    return jnp.concatenate([re * twist[0] - im * twist[1], re * twist[1] + im * twist[0]], axis=1)


def untwisted(value, twist):
    re, im = value[:, :N2], value[:, N2:]
    return jnp.concatenate([re * twist[0] + im * twist[1], im * twist[0] - re * twist[1]], axis=0)


def fused_kernel(
    scale, query_hbm, key_hbm, value_hbm, grad_hbm, taps_hbm, first_hbm, last_hbm, twist_hbm, mats_hbm, landed,
    inputs, taps, first_both, last_all, twist_ref, mats, packed, arrived, back, signals, filters, filter_spectra, spectra, results, sums, pair_sums, parts,
    load_sem, out_send, out_recv, back_send, back_recv, own_sem, pair_send, pair_recv, part_send, part_recv,
):
    z_hi, core, ctx = place()
    dp = z_hi * 2 + core
    pair = (z_hi * 2 + (core + 1) % 2, ctx)
    loads = [
        pltpu.make_async_copy(ref, inputs.at[i], load_sem.at[i])
        for i, ref in enumerate((key_hbm, value_hbm, grad_hbm, query_hbm))
    ]
    later = ((taps_hbm, taps), (first_hbm, first_both), (last_hbm, last_all), (twist_hbm, twist_ref), (mats_hbm, mats))
    loads += [pltpu.make_async_copy(ref, held, load_sem.at[4 + i]) for i, (ref, held) in enumerate(later)]
    for load in loads:
        load.start()

    barrier = pltpu.get_barrier_semaphore()

    xs = [((ctx // 8 + d) % 4) * 8 for d in range(4)]
    zs = [((ctx // 4 + d) % 2) * 4 for d in range(2)]
    ys = [(ctx + d) % 4 for d in range(4)]
    partners = [xs[dx] + zs[dz] + ys[dy] for dx, dz, dy in OFFSETS]
    for there in partners:
        pl.semaphore_signal(barrier, inc=1, device_id=(dp, there), device_id_type=MESH)
    pl.semaphore_signal(barrier, inc=1, device_id=pair, device_id_type=MESH)
    for away in range(1, 4):
        there = ((z_hi + away) % 4) * 2 + core
        pl.semaphore_signal(barrier, inc=1, device_id=(there, ctx), device_id_type=MESH)

    def out_copy(half, there):
        return pltpu.make_async_remote_copy(
            src_ref=packed.at[half, there],
            dst_ref=arrived.at[half, ctx],
            send_sem=out_send.at[half],
            recv_sem=out_recv.at[half],
            device_id=(dp, there),
            device_id_type=MESH,
        )

    def back_copy(half, there):
        return pltpu.make_async_remote_copy(
            src_ref=back.at[half, there],
            dst_ref=landed.at[half * N1 + ctx],
            send_sem=back_send.at[half],
            recv_sem=back_recv.at[half],
            device_id=(dp, there),
            device_id_type=MESH,
        )

    def wait_for(ref, sem):
        pltpu.make_async_copy(ref, ref, sem).wait()

    def pair_copy(half, z):
        return pltpu.make_async_remote_copy(
            src_ref=sums.at[half, pl.ds((z * 2 + (core + 1) % 2) * 64, 64)],
            dst_ref=pair_sums.at[half, z],
            send_sem=pair_send.at[half, z],
            recv_sem=pair_recv.at[half, z],
            device_id=pair,
            device_id_type=MESH,
        )

    def part_copy(half, there, slot):
        return pltpu.make_async_remote_copy(
            src_ref=parts.at[half, there],
            dst_ref=landed.at[pl.ds(2 * N1 + (half * 4 + slot) * 2, 2)],
            send_sem=part_send.at[half, there],
            recv_sem=part_recv.at[half, slot],
            device_id=(there * 2 + core, ctx),
            device_id_type=MESH,
        )

    for load in loads[:4]:
        load.wait()
    for block in range(8):
        lanes = slice(128 * block, 128 * block + 128)
        for array in range(2):
            gated = inputs[2 * array, :, lanes].astype(F32) * inputs[2 * array + 1, :, lanes].astype(F32)
            turned = gated.astype(BF16).T
            for part in range(8):
                packed[part % 2, 4 * block + part // 2, array] = turned[16 * part : 16 * part + 16]
    pl.semaphore_wait(barrier, 35)
    for there in partners:
        out_copy(0, there).start()
    own = [
        pltpu.make_async_copy(packed.at[half, ctx], arrived.at[half, ctx], out_recv.at[half]) for half in range(2)
    ]
    keep = [
        pltpu.make_async_copy(back.at[half, ctx], landed.at[half * N1 + ctx], back_recv.at[half]) for half in range(2)
    ] + [
        pltpu.make_async_copy(
            parts.at[half, z_hi], landed.at[pl.ds(2 * N1 + (half * 4 + z_hi) * 2, 2)], own_sem.at[half]
        )
        for half in range(2)
    ]
    own[0].start()
    own[1].start()
    for there in partners:
        out_copy(1, there).start()

    for load in loads[4:]:
        load.wait()
    twist = (twist_ref[0], twist_ref[1])
    for n1 in range(N1):
        filters[32 * n1 : 32 * n1 + 32] = taps[:, N2 * n1 : N2 * n1 + N2]

    def filter_work(group, carry):
        forward = []
        for item in range(0, GROUP, 2):
            rows = [filters[pl.ds(group * GROUP + item + i, N1, stride=32)] for i in range(2)]
            high, low = split(jnp.concatenate(rows, axis=1))
            left = first_both[...]
            out = dot(left, jnp.concatenate([high, high], axis=0)) + dot(left[:, :N1], low)
            forward += [twisted(out[:, :N2], twist), twisted(out[:, N2:], twist)]
        rows = pl.ds(pl.multiple_of(group * GROUP * N1, GROUP * N1), GROUP * N1)
        filter_spectra[rows] = middle(jnp.concatenate(forward, axis=0), mats.at[0])
        return carry

    lax.fori_loop(0, 2 * HALF // GROUP, filter_work, 0)

    def sum_parts(half):
        for z in range(4):
            pair_copy(half, z).wait()
            mine = sums[half, pl.ds(pl.multiple_of((z * 2 + core) * 64, 64), 64)]
            parts[half, z] = (mine + pair_sums[half, z]).astype(BF16).reshape(2, 2, HALF, N2)
        for away in (2, 1, 3):
            part_copy(half, (z_hi + away) % 4, z_hi).start()
        keep[2 + half].start()

    for half in range(2):
        wait_for(arrived.at[half], out_recv.at[half])

        def unpack(n1, carry):
            rows = arrived[half, n1].reshape(32, N2).astype(F32)
            signals[pl.ds(pl.multiple_of(n1 * 32, 32), 32)] = rows
            return carry

        lax.fori_loop(0, N1, unpack, 0, unroll=8)

        def spectrum(index):
            block = spectra[pl.ds(pl.multiple_of(index * N1, N1), N1)]
            return block[:, :N2], block[:, N2:]

        def finish(indices):
            turned = [untwisted(results[N1 * i : N1 * i + N1], twist) for i in indices]
            high, low = split(jnp.concatenate(turned, axis=1))
            out = dot(last_all[...], jnp.concatenate([high, low, high], axis=0))
            return out[:, :N2], out[:, N2:]

        def taps_work(group, carry):
            forward = []
            for item in range(GROUP):
                rows = [signals[pl.ds(group * GROUP + item + HALF * i, N1, stride=32)] for i in range(2)]
                data = jnp.concatenate(rows, axis=1).astype(BF16)
                out = dot(first_both[...], jnp.concatenate([data, data], axis=0))
                forward += [twisted(out[:, :N2], twist), twisted(out[:, N2:], twist)]
            rows = pl.ds(pl.multiple_of(group * 2 * GROUP * N1, 2 * GROUP * N1), 2 * GROUP * N1)
            spectra[rows] = middle(jnp.concatenate(forward, axis=0), mats.at[0])
            inverse = []
            for item in range(GROUP):
                u_re, u_im = spectrum(2 * (group * GROUP + item))
                m_re, m_im = spectrum(2 * (group * GROUP + item) + 1)
                inverse.append(jnp.concatenate([m_re * u_re + m_im * u_im, m_im * u_re - m_re * u_im], axis=1))
            results[: GROUP * N1] = middle(jnp.concatenate(inverse, axis=0), mats.at[1])
            for item in range(0, GROUP, 2):
                c = group * GROUP + item
                first, second = finish((item, item + 1))
                sums[half, pl.ds(c, N1, stride=HALF)] = first * scale
                sums[half, pl.ds(c + 1, N1, stride=HALF)] = second * scale
            return carry

        lax.fori_loop(0, HALF // GROUP, taps_work, 0)
        for z in range(4):
            pair_copy(half, z).start()
        if half == 1:
            sum_parts(0)

        def work(group, carry):
            inverse = []
            for item in range(GROUP):
                start = (half * HALF + group * GROUP + item) * N1
                h = filter_spectra[pl.ds(pl.multiple_of(start, N1), N1)]
                h_re, h_im = h[:, :N2], h[:, N2:]
                u_re, u_im = spectrum(2 * (group * GROUP + item))
                m_re, m_im = spectrum(2 * (group * GROUP + item) + 1)
                inverse.append(jnp.concatenate([h_re * u_re - h_im * u_im, h_re * u_im + h_im * u_re], axis=1))
                inverse.append(jnp.concatenate([m_re * h_re + m_im * h_im, m_im * h_re - m_re * h_im], axis=1))
            results[...] = middle(jnp.concatenate(inverse, axis=0), mats.at[1])
            for item in range(GROUP):
                c = group * GROUP + item
                conv, inner = finish((2 * item, 2 * item + 1))
                signals[pl.ds(c, N1, stride=32)] = conv
                signals[pl.ds(c + HALF, N1, stride=32)] = inner
            return carry

        lax.fori_loop(0, HALF // GROUP, work, 0)

        def pack(n1, carry):
            rows = signals[pl.ds(pl.multiple_of(n1 * 32, 32), 32)].astype(BF16)
            back[half, n1] = rows.reshape(2, 16, N2)
            return carry

        lax.fori_loop(0, N1, pack, 0, unroll=8)
        for there in partners:
            back_copy(half, there).start()
        keep[half].start()
        if half == 1:
            sum_parts(half)

    for half in range(2):
        wait_for(packed.at[half, pl.ds(0, N1 - 1)], out_send.at[half])
        wait_for(back.at[half, pl.ds(0, N1 - 1)], back_send.at[half])
        wait_for(landed.at[pl.ds(half * N1, N1)], back_recv.at[half])
        keep[2 + half].wait()
        for away in (2, 1, 3):
            there = (z_hi + away) % 4
            part_copy(half, there, there).wait()


def gate_kernel(landed, query, key, value, grad, query_grad, key_grad, value_grad, taps_grad):
    for block in range(8):
        lanes = slice(128 * block, 128 * block + 128)
        slots = [half * N1 + 4 * block + device for device in range(4) for half in range(2)]
        conv = jnp.concatenate([landed[slot, 0] for slot in slots], axis=0).astype(F32).T
        inner = jnp.concatenate([landed[slot, 1] for slot in slots], axis=0).astype(F32).T
        query_grad[:, lanes] = (conv * grad[:, lanes].astype(F32)).astype(BF16)
        key_grad[:, lanes] = (inner * value[:, lanes].astype(F32)).astype(BF16)
        value_grad[:, lanes] = (inner * key[:, lanes].astype(F32)).astype(BF16)
    for half in range(2):
        pieces = [2 * N1 + (4 * half + z) * 2 for z in range(4)]
        total = landed[pieces[0] : pieces[0] + 2].reshape(4 * HALF, N2).astype(F32)
        for piece in pieces[1:]:
            total = total + landed[piece : piece + 2].reshape(4 * HALF, N2).astype(F32)
        for n1 in range(4):
            taps_grad[16 * half : 16 * half + 16, N2 * n1 : N2 * n1 + N2] = total[16 * n1 : 16 * n1 + 16]


def on_device(query_proj, key_proj, value_proj, out_grad, filter_taps):
    rows = query_proj.shape[1]
    query, key, value, grad = (a.reshape(rows, -1) for a in (query_proj, key_proj, value_proj, out_grad))
    vmem = pl.BlockSpec(memory_space=pltpu.VMEM)
    anywhere = pl.BlockSpec(memory_space=pl.ANY)
    limit = 62 * 1024 * 1024
    slabs = (2, N1, 2, HALF, N2)
    scale = 1.0 / math.sqrt(lax.axis_size("dp") * LENGTH)
    dma = pltpu.SemaphoreType.DMA
    landed = pl.pallas_call(
        functools.partial(fused_kernel, scale),
        out_shape=jax.ShapeDtypeStruct((2 * N1 + 16, 2, HALF, N2), BF16),
        in_specs=[anywhere] * 9,
        out_specs=anywhere,
        scratch_shapes=[
            pltpu.VMEM((4, rows, query.shape[1]), BF16),
            pltpu.VMEM((2 * HALF, LENGTH), F32),
            pltpu.VMEM((2 * N1, 2 * N1), BF16),
            pltpu.VMEM((N1, 6 * N1), BF16),
            pltpu.VMEM((2, N1, N2), F32),
            pltpu.VMEM((2, 6 * N2, 2 * N2), BF16),
            pltpu.VMEM(slabs, BF16),
            pltpu.VMEM(slabs, BF16),
            pltpu.VMEM(slabs, BF16),
            pltpu.VMEM((N1 * 2 * HALF, N2), F32),
            pltpu.VMEM((N1 * 2 * HALF, N2), F32),
            pltpu.VMEM((2 * HALF * N1, 2 * N2), F32),
            pltpu.VMEM((2 * HALF * N1, 2 * N2), F32),
            pltpu.VMEM((2 * GROUP * N1, 2 * N2), F32),
            pltpu.VMEM((2, N1 * HALF, N2), F32),
            pltpu.VMEM((2, 4, 64, N2), F32),
            pltpu.VMEM((2, 4, 2, 2, HALF, N2), BF16),
            dma((9,)),
            dma((2,)),
            dma((2,)),
            dma((2,)),
            dma((2,)),
            dma((2,)),
            dma((2, 4)),
            dma((2, 4)),
            dma((2, 4)),
            dma((2, 4)),
        ],
        compiler_params=pltpu.CompilerParams(collective_id=0, has_side_effects=True, vmem_limit_bytes=limit),
        name="exchange_convolve",
    )(query, key, value, grad, filter_taps.T, *(jnp.asarray(t) for t in tables()))
    flat = jax.ShapeDtypeStruct(query.shape, BF16)
    outs = pl.pallas_call(
        gate_kernel,
        out_shape=(flat, flat, flat, jax.ShapeDtypeStruct((2 * HALF, 4 * N2), F32)),
        in_specs=[vmem] * 5,
        out_specs=(vmem,) * 4,
        compiler_params=pltpu.CompilerParams(vmem_limit_bytes=48 * 1024 * 1024),
        name="gate",
    )(landed, query, key, value, grad)
    return tuple(o.reshape(query_proj.shape) for o in outs[:3]) + (outs[3].T,)


def solution(mesh):
    placed = (P("dp", "ctx", None),) * 4 + (P(None, "ctx"),)
    return jax.shard_map(
        on_device,
        mesh=mesh,
        in_specs=placed,
        out_specs=(P("dp", "ctx", None),) * 3 + (P("dp", "ctx"),),
        check_vma=False,
    )
```

```python
import functools
import math

import jax
import jax.numpy as jnp
import ml_dtypes
import numpy as np
from jax import lax
from jax.experimental import pallas as pl
from jax.experimental.pallas import tpu as pltpu
from jax.sharding import PartitionSpec as P

MESH = pl.DeviceIdType.MESH
F32 = jnp.float32
BF16 = jnp.bfloat16

N1 = 32
N2 = 128
LENGTH = N1 * N2
GROUP = 16
HALF = 16


def high_low(table):
    high = table.astype(ml_dtypes.bfloat16)
    low = (table - high.astype(np.float64)).astype(ml_dtypes.bfloat16)
    return high, low


@functools.lru_cache(maxsize=None)
def tables():
    row = np.arange(N1)
    col = np.arange(N2)
    outer = 2 * np.pi * np.outer(row + 0.25, row) / N1
    first = np.concatenate([np.cos(outer), -np.sin(outer)], axis=0)
    first_high, first_low = high_low(first)
    first_both = np.concatenate([first_high, first_low], axis=1)
    last = np.concatenate([np.cos(outer.T), -np.sin(outer.T)], axis=1) / LENGTH
    last_high, last_low = high_low(last)
    none = np.zeros_like(last_high)
    last_all = np.block(
        [
            [last_high, last_high, none, none],
            [none, none, last_high, last_high],
            [last_low, none, none, none],
            [none, none, last_low, none],
        ]
    )
    turn = 2 * np.pi * np.outer(row + 0.25, col) / LENGTH
    twist = np.stack([np.cos(turn), -np.sin(turn)]).astype(np.float32)
    inner = 2 * np.pi * (np.outer(col, col) % N2) / N2
    cos, sin = np.cos(inner), np.sin(inner)
    forward = np.block([[cos, -sin], [sin, cos]])
    inverse = np.block([[cos, sin], [-sin, cos]])
    stacked = []
    for matrix in (forward, inverse):
        high, low = high_low(matrix)
        stacked.append(np.concatenate([high, high, low], axis=0))
    stacked = np.stack(stacked)
    return first_both, last_all, twist, stacked


def place():
    dp = lax.axis_index("dp")
    ctx = lax.axis_index("ctx")
    return dp // 2, dp % 2, ctx


OFFSETS = sorted(
    ((dx, dz, dy) for dx in range(4) for dz in range(2) for dy in range(4) if dx or dz or dy),
    key=lambda o: -(min(o[0], 4 - o[0]) + o[1] + min(o[2], 4 - o[2])),
)


def split(value):
    high = value.astype(BF16)
    return high, (value - high.astype(F32)).astype(BF16)


def dot(left, right):
    return lax.dot_general(left, right, (((1,), (0,)), ((), ())), preferred_element_type=F32)


def middle(value, stacked):
    high, low = split(value)
    return dot(jnp.concatenate([high, low, high], axis=1), stacked[...])


def twisted(value, twist):
    re, im = value[:N1], value[N1:]
    return jnp.concatenate([re * twist[0] - im * twist[1], re * twist[1] + im * twist[0]], axis=1)


def untwisted(value, twist):
    re, im = value[:, :N2], value[:, N2:]
    return jnp.concatenate([re * twist[0] + im * twist[1], im * twist[0] - re * twist[1]], axis=0)


def fused_kernel(
    scale, query_hbm, key_hbm, value_hbm, grad_hbm, taps_hbm, first_hbm, last_hbm, twist_hbm, mats_hbm, landed,
    inputs, taps, first_both, last_all, twist_ref, mats, packed, arrived, back, signals, filters, filter_spectra, spectra, results, sums, pair_sums, parts,
    load_sem, out_send, out_recv, back_send, back_recv, own_sem, pair_send, pair_recv, part_send, part_recv,
):
    z_hi, core, ctx = place()
    dp = z_hi * 2 + core
    pair = (z_hi * 2 + (core + 1) % 2, ctx)
    loads = [
        pltpu.make_async_copy(ref, inputs.at[i], load_sem.at[i])
        for i, ref in enumerate((key_hbm, value_hbm, grad_hbm, query_hbm))
    ]
    later = ((taps_hbm, taps), (first_hbm, first_both), (last_hbm, last_all), (twist_hbm, twist_ref), (mats_hbm, mats))
    loads += [pltpu.make_async_copy(ref, held, load_sem.at[4 + i]) for i, (ref, held) in enumerate(later)]
    for load in loads:
        load.start()

    barrier = pltpu.get_barrier_semaphore()

    xs = [((ctx // 8 + d) % 4) * 8 for d in range(4)]
    zs = [((ctx // 4 + d) % 2) * 4 for d in range(2)]
    ys = [(ctx + d) % 4 for d in range(4)]
    partners = [xs[dx] + zs[dz] + ys[dy] for dx, dz, dy in OFFSETS]
    for there in partners:
        pl.semaphore_signal(barrier, inc=1, device_id=(dp, there), device_id_type=MESH)
    pl.semaphore_signal(barrier, inc=1, device_id=pair, device_id_type=MESH)
    for away in range(1, 4):
        there = ((z_hi + away) % 4) * 2 + core
        pl.semaphore_signal(barrier, inc=1, device_id=(there, ctx), device_id_type=MESH)

    def out_copy(half, there):
        return pltpu.make_async_remote_copy(
            src_ref=packed.at[half, there],
            dst_ref=arrived.at[half, ctx],
            send_sem=out_send.at[half],
            recv_sem=out_recv.at[half],
            device_id=(dp, there),
            device_id_type=MESH,
        )

    def back_copy(half, there):
        return pltpu.make_async_remote_copy(
            src_ref=back.at[half, there],
            dst_ref=landed.at[half * N1 + ctx],
            send_sem=back_send.at[half],
            recv_sem=back_recv.at[half],
            device_id=(dp, there),
            device_id_type=MESH,
        )

    def wait_for(ref, sem):
        pltpu.make_async_copy(ref, ref, sem).wait()

    def pair_copy(half, z):
        return pltpu.make_async_remote_copy(
            src_ref=sums.at[half, pl.ds((z * 2 + (core + 1) % 2) * 64, 64)],
            dst_ref=pair_sums.at[half, z],
            send_sem=pair_send.at[half, z],
            recv_sem=pair_recv.at[half, z],
            device_id=pair,
            device_id_type=MESH,
        )

    def part_copy(half, there, slot):
        return pltpu.make_async_remote_copy(
            src_ref=parts.at[half, there],
            dst_ref=landed.at[pl.ds(2 * N1 + (half * 4 + slot) * 2, 2)],
            send_sem=part_send.at[half, there],
            recv_sem=part_recv.at[half, slot],
            device_id=(there * 2 + core, ctx),
            device_id_type=MESH,
        )

    for load in loads[:4]:
        load.wait()
    for block in range(8):
        lanes = slice(128 * block, 128 * block + 128)
        for array in range(2):
            gated = inputs[2 * array, :, lanes].astype(F32) * inputs[2 * array + 1, :, lanes].astype(F32)
            turned = gated.astype(BF16).T
            for part in range(8):
                packed[part % 2, 4 * block + part // 2, array] = turned[16 * part : 16 * part + 16]
    pl.semaphore_wait(barrier, 35)
    for there in partners:
        out_copy(0, there).start()
    own = [
        pltpu.make_async_copy(packed.at[half, ctx], arrived.at[half, ctx], out_recv.at[half]) for half in range(2)
    ]
    keep = [
        pltpu.make_async_copy(back.at[half, ctx], landed.at[half * N1 + ctx], back_recv.at[half]) for half in range(2)
    ] + [
        pltpu.make_async_copy(
            parts.at[half, z_hi], landed.at[pl.ds(2 * N1 + (half * 4 + z_hi) * 2, 2)], own_sem.at[half]
        )
        for half in range(2)
    ]
    own[0].start()
    own[1].start()
    for there in partners:
        out_copy(1, there).start()

    for load in loads[4:]:
        load.wait()
    twist = (twist_ref[0], twist_ref[1])
    for n1 in range(N1):
        filters[32 * n1 : 32 * n1 + 32] = taps[:, N2 * n1 : N2 * n1 + N2]

    def filter_work(group, carry):
        forward = []
        for item in range(0, GROUP, 2):
            rows = [filters[pl.ds(group * GROUP + item + i, N1, stride=32)] for i in range(2)]
            high, low = split(jnp.concatenate(rows, axis=1))
            left = first_both[...]
            out = dot(left, jnp.concatenate([high, high], axis=0)) + dot(left[:, :N1], low)
            forward += [twisted(out[:, :N2], twist), twisted(out[:, N2:], twist)]
        rows = pl.ds(pl.multiple_of(group * GROUP * N1, GROUP * N1), GROUP * N1)
        filter_spectra[rows] = middle(jnp.concatenate(forward, axis=0), mats.at[0])
        return carry

    lax.fori_loop(0, 2 * HALF // GROUP, filter_work, 0)

    def sum_parts(half):
        for z in range(4):
            pair_copy(half, z).wait()
            mine = sums[half, pl.ds(pl.multiple_of((z * 2 + core) * 64, 64), 64)]
            parts[half, z] = (mine + pair_sums[half, z]).astype(BF16).reshape(2, 2, HALF, N2)
        for away in (2, 1, 3):
            part_copy(half, (z_hi + away) % 4, z_hi).start()
        keep[2 + half].start()

    for half in range(2):
        wait_for(arrived.at[half], out_recv.at[half])

        for n1 in range(N1):
            signals[33 * n1 : 33 * n1 + 32] = arrived[half, n1].reshape(32, N2).astype(F32)

        def spectrum(index):
            block = spectra[pl.ds(pl.multiple_of(index * N1, N1), N1)]
            return block[:, :N2], block[:, N2:]

        def finish(indices):
            data = []
            for pair in (indices[:2], indices[2:]):
                turned = [untwisted(results[N1 * i : N1 * i + N1], twist) for i in pair]
                data += split(jnp.concatenate(turned, axis=1))
            out = dot(last_all[...], jnp.concatenate(data, axis=0))
            out = out[: 2 * N1] + out[2 * N1 :]
            return out[:N1, :N2], out[:N1, N2:], out[N1:, :N2], out[N1:, N2:]

        def taps_work(group, carry):
            forward = []
            for item in range(GROUP):
                rows = [signals[pl.ds(group * GROUP + item + HALF * i, N1, stride=33)] for i in range(2)]
                data = jnp.concatenate(rows, axis=1).astype(BF16)
                out = dot(first_both[...], jnp.concatenate([data, data], axis=0))
                forward += [twisted(out[:, :N2], twist), twisted(out[:, N2:], twist)]
            rows = pl.ds(pl.multiple_of(group * 2 * GROUP * N1, 2 * GROUP * N1), 2 * GROUP * N1)
            spectra[rows] = middle(jnp.concatenate(forward, axis=0), mats.at[0])
            inverse = []
            for item in range(GROUP):
                u_re, u_im = spectrum(2 * (group * GROUP + item))
                m_re, m_im = spectrum(2 * (group * GROUP + item) + 1)
                inverse.append(jnp.concatenate([m_re * u_re + m_im * u_im, m_im * u_re - m_re * u_im], axis=1))
            results[: GROUP * N1] = middle(jnp.concatenate(inverse, axis=0), mats.at[1])
            for item in range(0, GROUP, 4):
                c = group * GROUP + item
                for i, rows in enumerate(finish((item, item + 1, item + 2, item + 3))):
                    sums[half, pl.ds(c + i, N1, stride=HALF)] = rows * scale
            return carry

        lax.fori_loop(0, HALF // GROUP, taps_work, 0)
        for z in range(4):
            pair_copy(half, z).start()
        if half == 1:
            sum_parts(0)

        def work(group, carry):
            inverse = []
            for item in range(GROUP):
                start = (half * HALF + group * GROUP + item) * N1
                h = filter_spectra[pl.ds(pl.multiple_of(start, N1), N1)]
                h_re, h_im = h[:, :N2], h[:, N2:]
                u_re, u_im = spectrum(2 * (group * GROUP + item))
                m_re, m_im = spectrum(2 * (group * GROUP + item) + 1)
                inverse.append(jnp.concatenate([h_re * u_re - h_im * u_im, h_re * u_im + h_im * u_re], axis=1))
                inverse.append(jnp.concatenate([m_re * h_re + m_im * h_im, m_im * h_re - m_re * h_im], axis=1))
            results[...] = middle(jnp.concatenate(inverse, axis=0), mats.at[1])
            for item in range(0, GROUP, 2):
                c = group * GROUP + item
                done = finish((2 * item, 2 * item + 1, 2 * item + 2, 2 * item + 3))
                for i in range(2):
                    signals[pl.ds(c + i, N1, stride=33)] = done[2 * i]
                    signals[pl.ds(c + i + HALF, N1, stride=33)] = done[2 * i + 1]
            return carry

        lax.fori_loop(0, HALF // GROUP, work, 0)

        for n1 in range(N1):
            back[half, n1] = signals[33 * n1 : 33 * n1 + 32].astype(BF16).reshape(2, 16, N2)
        for there in partners[:20]:
            back_copy(half, there).start()
        if half == 1:
            sum_parts(half)
        for there in partners[20:]:
            back_copy(half, there).start()
        keep[half].start()

    for half in range(2):
        wait_for(packed.at[half, pl.ds(0, N1 - 1)], out_send.at[half])
        wait_for(back.at[half, pl.ds(0, N1 - 1)], back_send.at[half])
        wait_for(landed.at[pl.ds(half * N1, N1)], back_recv.at[half])
        keep[2 + half].wait()
        for away in (2, 1, 3):
            there = (z_hi + away) % 4
            part_copy(half, there, there).wait()


def gate_kernel(landed, query, key, value, grad, query_grad, key_grad, value_grad, taps_grad):
    for block in range(8):
        lanes = slice(128 * block, 128 * block + 128)
        slots = [half * N1 + 4 * block + device for device in range(4) for half in range(2)]
        conv = jnp.concatenate([landed[slot, 0] for slot in slots], axis=0).astype(F32).T
        inner = jnp.concatenate([landed[slot, 1] for slot in slots], axis=0).astype(F32).T
        query_grad[:, lanes] = (conv * grad[:, lanes].astype(F32)).astype(BF16)
        key_grad[:, lanes] = (inner * value[:, lanes].astype(F32)).astype(BF16)
        value_grad[:, lanes] = (inner * key[:, lanes].astype(F32)).astype(BF16)
    for half in range(2):
        pieces = [2 * N1 + (4 * half + z) * 2 for z in range(4)]
        total = landed[pieces[0] : pieces[0] + 2].reshape(4 * HALF, N2).astype(F32)
        for piece in pieces[1:]:
            total = total + landed[piece : piece + 2].reshape(4 * HALF, N2).astype(F32)
        for n1 in range(4):
            taps_grad[16 * half : 16 * half + 16, N2 * n1 : N2 * n1 + N2] = total[16 * n1 : 16 * n1 + 16]


def on_device(query_proj, key_proj, value_proj, out_grad, filter_taps):
    rows = query_proj.shape[1]
    query, key, value, grad = (a.reshape(rows, -1) for a in (query_proj, key_proj, value_proj, out_grad))
    vmem = pl.BlockSpec(memory_space=pltpu.VMEM)
    anywhere = pl.BlockSpec(memory_space=pl.ANY)
    limit = 62 * 1024 * 1024
    slabs = (2, N1, 2, HALF, N2)
    scale = 1.0 / math.sqrt(lax.axis_size("dp") * LENGTH)
    dma = pltpu.SemaphoreType.DMA
    landed = pl.pallas_call(
        functools.partial(fused_kernel, scale),
        out_shape=jax.ShapeDtypeStruct((2 * N1 + 16, 2, HALF, N2), BF16),
        in_specs=[anywhere] * 9,
        out_specs=anywhere,
        scratch_shapes=[
            pltpu.VMEM((4, rows, query.shape[1]), BF16),
            pltpu.VMEM((2 * HALF, LENGTH), F32),
            pltpu.VMEM((2 * N1, 2 * N1), BF16),
            pltpu.VMEM((4 * N1, 8 * N1), BF16),
            pltpu.VMEM((2, N1, N2), F32),
            pltpu.VMEM((2, 6 * N2, 2 * N2), BF16),
            pltpu.VMEM(slabs, BF16),
            pltpu.VMEM(slabs, BF16),
            pltpu.VMEM(slabs, BF16),
            pltpu.VMEM((N1 * (2 * HALF + 1), N2), F32),
            pltpu.VMEM((N1 * 2 * HALF, N2), F32),
            pltpu.VMEM((2 * HALF * N1, 2 * N2), F32),
            pltpu.VMEM((2 * HALF * N1, 2 * N2), F32),
            pltpu.VMEM((2 * GROUP * N1, 2 * N2), F32),
            pltpu.VMEM((2, N1 * HALF, N2), F32),
            pltpu.VMEM((2, 4, 64, N2), F32),
            pltpu.VMEM((2, 4, 2, 2, HALF, N2), BF16),
            dma((9,)),
            dma((2,)),
            dma((2,)),
            dma((2,)),
            dma((2,)),
            dma((2,)),
            dma((2, 4)),
            dma((2, 4)),
            dma((2, 4)),
            dma((2, 4)),
        ],
        compiler_params=pltpu.CompilerParams(collective_id=0, has_side_effects=True, vmem_limit_bytes=limit),
        name="exchange_convolve",
    )(query, key, value, grad, filter_taps.T, *(jnp.asarray(t) for t in tables()))
    flat = jax.ShapeDtypeStruct(query.shape, BF16)
    outs = pl.pallas_call(
        gate_kernel,
        out_shape=(flat, flat, flat, jax.ShapeDtypeStruct((2 * HALF, 4 * N2), F32)),
        in_specs=[vmem] * 5,
        out_specs=(vmem,) * 4,
        compiler_params=pltpu.CompilerParams(vmem_limit_bytes=48 * 1024 * 1024),
        name="gate",
    )(landed, query, key, value, grad)
    return tuple(o.reshape(query_proj.shape) for o in outs[:3]) + (outs[3].T,)


def solution(mesh):
    placed = (P("dp", "ctx", None),) * 4 + (P(None, "ctx"),)
    return jax.shard_map(
        on_device,
        mesh=mesh,
        in_specs=placed,
        out_specs=(P("dp", "ctx", None),) * 3 + (P("dp", "ctx"),),
        check_vma=False,
    )
```
